32 devices in a mesh: ctx: 8 (over y, x, core), fsdp: 4 (over z).
Axes of the slice: x: 2, y: 2, z: 4, core: 2. Of those that a mesh axis runs over, the one named last changes fastest.
Arguments:
- tokens: bfloat16 [4, 2048, 2048], P('fsdp', 'ctx'), may hold values from -6 to 6
- qkv_weight: bfloat16 [3, 2048, 2048], P(None, None, 'fsdp'), may hold values from -0.125 to 0.125
- log_decay: float32 [4, 16, 2048], P('fsdp', None, 'ctx'), may hold values from -3 to 0
- norm_gain: float32 [2048], replicated, may hold values from 0.25 to 1.75
Outputs:
- normed: bfloat16 [4, 2048, 2048], P('fsdp', 'ctx')
The draws below stay inside these ranges and needn't reach their ends.
All inputs are finite; a program needn't handle non-finite values.
Results may differ from the reference program's by a relative error of at most 0.009.
Values may be sent and summed in bfloat16 or wider, within the bound.
A program may use at most 192 MiB of HBM per device.

```python
import math
from functools import partial
import jax
import jax.numpy as jnp
from jax import lax

D = 2048
HEADS = 16
HEAD_DIM = 128
TOK_DEV = 256
TOKENS = 2048
SEQS = 4
INNER = 2048
N_CTX = 8


def draw_log_decay(key, part):
    keys_all = jax.random.split(jax.random.fold_in(key, 7), 5)
    slow_share = 0.5
    slow_heads = jax.random.uniform(keys_all[0], (SEQS, HEADS, 1), jnp.float32) < slow_share
    base_rate = jnp.where(slow_heads, 0.5 / TOKENS, 1.0 / 40.0)
    block_factor = jnp.exp(jax.random.uniform(keys_all[1], (SEQS, HEADS, TOKENS // TOK_DEV, 1), jnp.float32, math.log(0.5), math.log(2.0)))
    rough = jax.random.uniform(keys_all[2], (SEQS, HEADS, TOKENS // TOK_DEV, TOK_DEV), jnp.float32, 0.5, 1.5)
    constant_forget_factor = (rough * block_factor).reshape(SEQS, HEADS, TOKENS) * base_rate
    spots = jax.random.randint(keys_all[3], (SEQS, HEADS, 3, 1), 0, TOKENS)
    forget_strength_levels = jax.random.uniform(keys_all[4], (SEQS, HEADS, 3, 1), jnp.float32, math.log(0.5), math.log(0.8))
    forget_event_positions = jnp.arange(TOKENS, dtype=jnp.int32)[None, None, None, :] == spots
    forget_spike_groups = jnp.sum(jnp.where(forget_event_positions, forget_strength_levels, 0.0), axis=2)
    return (forget_spike_groups - constant_forget_factor).astype(jnp.float32)


def steps_of(stream_key, extent, pieces, low, largest):
    level, own = 1.0, jax.random.fold_in(stream_key, 6)
    for axis_at, blocks in pieces:
        heights = jnp.exp(jax.random.uniform(jax.random.fold_in(own, axis_at), (blocks,), jnp.float32, low / len(pieces), largest / len(pieces)))
        level = level * jnp.repeat(heights, extent[axis_at] // blocks).reshape([-1 if axis == axis_at else 1 for axis in range(len(extent))])
    return level


def noise(key, shape, scale, reach, shards=(), kind=jnp.bfloat16):
    loudness = steps_of(key, shape, shards, -0.22, 0.18) if shards else 1.0
    array = jax.random.normal(key, shape, jnp.float32) * scale * loudness
    return jnp.minimum(jnp.maximum(array, -reach), reach).astype(kind)


def setup_inputs(seed: int = 0) -> dict:
    streams_of = jax.random.split(jax.random.key(seed), 5)
    tokens = noise(streams_of[0], (SEQS, TOKENS, D), 1.0, 6.0, ((0, 4), (1, 8)))
    qkv_weight = noise(streams_of[1], (3, D, INNER), D ** -0.5, 0.125, ((2, 4),))
    log_decay = draw_log_decay(jax.random.fold_in(streams_of[4], 71), 0)
    norm_gain = jnp.clip(1.0 + 0.15 * jax.random.normal(streams_of[3], (INNER,), jnp.float32), 0.25, 1.75)
    return dict(tokens=tokens, qkv_weight=qkv_weight, log_decay=log_decay, norm_gain=norm_gain)


def block_step(state, packed, qkv_weight, norm_gain):
    block_in, rates = packed
    projected = [jnp.dot(block_in, qkv_weight[index], preferred_element_type=jnp.float32) for index in range(3)]
    queries = jax.nn.silu(projected[0]).astype(jnp.bfloat16).reshape(TOK_DEV, HEADS, HEAD_DIM)
    keys = jax.nn.silu(projected[1]).astype(jnp.bfloat16).reshape(TOK_DEV, HEADS, HEAD_DIM)
    values = projected[2].astype(jnp.bfloat16).reshape(TOK_DEV, HEADS, HEAD_DIM)
    cumulative = jnp.cumsum(rates, axis=1)
    log_gaps = cumulative[:, :, None] - cumulative[:, None, :]
    causal = jnp.arange(TOK_DEV)[:, None] >= jnp.arange(TOK_DEV)[None, :]
    factors = jnp.exp(jnp.where(causal[None], log_gaps, -jnp.inf))
    scores = jnp.einsum('thd,shd->hts', queries.astype(jnp.float32), keys.astype(jnp.float32))
    weights = (scores * factors).astype(jnp.bfloat16)
    inside = jnp.einsum('hts,shd->thd', weights.astype(jnp.float32), values.astype(jnp.float32))
    reduced_precision_memory = lax.optimization_barrier(state.astype(jnp.bfloat16))
    incoming = jnp.einsum('thd,hde->the', queries.astype(jnp.float32), reduced_precision_memory.astype(jnp.float32))
    incoming = incoming * jnp.exp(cumulative).T[:, :, None]
    attention_output = (inside + incoming).reshape(TOK_DEV, HEADS * HEAD_DIM)
    mean_sq = lax.optimization_barrier(jnp.mean(attention_output * attention_output, axis=-1, keepdims=True))
    normed = (attention_output * lax.rsqrt(mean_sq + 1e-05) * norm_gain).astype(jnp.bfloat16)
    tail = jnp.exp(cumulative[:, -1:] - cumulative)
    weighted_key_vectors = lax.optimization_barrier((keys.astype(jnp.float32) * tail.T[:, :, None]).astype(jnp.bfloat16))
    local = jnp.einsum('thd,the->hde', weighted_key_vectors.astype(jnp.float32), values.astype(jnp.float32))
    decay_total = jnp.exp(cumulative[:, -1])
    new_state = decay_total[:, None, None] * state + local
    return (new_state, normed)

def reference(tokens, qkv_weight, log_decay, norm_gain):

    def one_sequence(packed):
        seq_tokens, seq_rates = packed
        blocks = seq_tokens.reshape(N_CTX, TOK_DEV, D)
        rate_blocks = seq_rates.reshape(HEADS, N_CTX, TOK_DEV).transpose(1, 0, 2)
        initial = jnp.zeros((HEADS, HEAD_DIM, HEAD_DIM), jnp.float32)
        stepper = partial(block_step, qkv_weight=qkv_weight, norm_gain=norm_gain)
        last_state, outputs = lax.scan(stepper, initial, (blocks, rate_blocks))
        return outputs.reshape(TOKENS, HEADS * HEAD_DIM)
    return lax.map(one_sequence, (tokens, log_decay))
```

```python
import functools
import jax
import jax.numpy as jnp
from jax import lax
from jax.experimental import pallas as pl
from jax.experimental.pallas import tpu as pltpu
from jax.sharding import PartitionSpec as P

MESH = pl.DeviceIdType.MESH
CUBE = 8
CHUNKS = 4
F32 = jnp.float32
BF16 = jnp.bfloat16


def flip(c, r):
    out = c
    bit = 1
    while bit < CUBE:
        if r & bit:
            out = out + bit - 2 * bit * ((c // bit) % 2)
        bit *= 2
    return out


def head_kernel(
    dims,
    tok_in,
    w_in,
    cum_in,
    gain_ref,
    out_ref,
    tok,
    w,
    cums,
    stage,
    gat,
    state,
    local_sem,
    tok_send,
    tok_recv,
    w_up,
    w_down,
    w_recv,
    cum_send,
    cum_recv,
    out_send,
    out_recv,
):
    n_fsdp, shard_heads, per_dev, hd, feats = dims
    groups = n_fsdp // per_dev
    c = lax.axis_index("ctx")
    f = lax.axis_index("fsdp")
    j, a = c // groups, c % groups
    rows = tok.shape[1]
    half = rows // 2
    depth = w.shape[1]
    step = depth // CHUNKS

    first = jnp.where(f > a * per_dev, 1, 0)

    own_tok = pltpu.make_async_copy(tok_in, tok.at[c], local_sem.at[0])
    own_tok.start()
    own_cum = pltpu.make_async_copy(cum_in, cums.at[c], local_sem.at[1])
    own_cum.start()
    owner = f // per_dev == a
    own_i = f % per_dev

    def own_weight(p):
        return pltpu.make_async_copy(
            w_in.at[p, :, pl.ds(pl.multiple_of(j * hd, hd), hd)],
            w.at[own_i, :, pl.ds(p * hd, hd)],
            local_sem.at[2 + p],
        )

    @pl.when(owner)
    def _():
        for p in range(3):
            own_weight(p).start()

    barrier = pltpu.get_barrier_semaphore()
    for r in range(1, CUBE):
        pl.semaphore_signal(barrier, inc=1, device_id={"ctx": flip(c, r)}, device_id_type=MESH)

    @pl.when(f > 0)
    def _():
        pl.semaphore_signal(barrier, inc=1, device_id={"fsdp": f - 1}, device_id_type=MESH)

    @pl.when(f < n_fsdp - 1)
    def _():
        pl.semaphore_signal(barrier, inc=1, device_id={"fsdp": f + 1}, device_id_type=MESH)

    ends = jnp.where(f > 0, 1, 0) + jnp.where(f < n_fsdp - 1, 1, 0)
    pl.semaphore_wait(barrier, CUBE - 1 + ends)

    def tok_copy(r, p, d):
        part = tok.at[flip(c, r), pl.ds(p * half, half), :]
        return pltpu.make_async_remote_copy(
            src_ref=part,
            dst_ref=part,
            send_sem=tok_send.at[r, p, (1, 2, 4).index(d)],
            recv_sem=tok_recv.at[r ^ d, p],
            device_id={"ctx": flip(c, d)},
            device_id_type=MESH,
        )

    def tok_wait(r, p):
        part = tok.at[flip(c, r), pl.ds(p * half, half), :]
        pltpu.make_async_remote_copy(
            src_ref=part,
            dst_ref=part,
            send_sem=tok_send.at[r, p, 0],
            recv_sem=tok_recv.at[r, p],
            device_id={"ctx": flip(c, 1)},
            device_id_type=MESH,
        ).wait_recv()

    sent = []

    def tok_start(r, p, d):
        copy = tok_copy(r, p, d)
        copy.start()
        sent.append(copy)

    def w_copy(i, k, up):
        part = w.at[i, pl.ds(pl.multiple_of(k * step, step), step), :]
        return pltpu.make_async_remote_copy(
            src_ref=part,
            dst_ref=part,
            send_sem=(w_up if up else w_down).at[i, k],
            recv_sem=w_recv.at[i, k],
            device_id={"fsdp": f + 1 if up else f - 1},
            device_id_type=MESH,
        )

    def goes_up(i):
        return jnp.logical_and(a * per_dev + i <= f, f < n_fsdp - 1)

    def goes_down(i):
        return jnp.logical_and(a * per_dev + i >= f, f > 0)

    def w_pass(i, k):
        @pl.when(a * per_dev + i < f)
        def _():
            w_copy(i, k, False).wait_recv()

        @pl.when(a * per_dev + i > f)
        def _():
            w_copy(i, k, True).wait_recv()

        @pl.when(goes_up(i))
        def _():
            w_copy(i, k, True).start()

        @pl.when(goes_down(i))
        def _():
            w_copy(i, k, False).start()

    def cum_copy(r):
        return pltpu.make_async_remote_copy(
            src_ref=cums.at[c],
            dst_ref=cums.at[c],
            send_sem=cum_send.at[r],
            recv_sem=cum_recv.at[r],
            device_id={"ctx": flip(c, r)},
            device_id_type=MESH,
        )

    @pl.when(owner)
    def _():
        for p in range(3):
            own_weight(p).wait()
        for k in range(CHUNKS):

            @pl.when(f < n_fsdp - 1)
            def _():
                w_copy(own_i, k, True).start()

            @pl.when(f > 0)
            def _():
                w_copy(own_i, k, False).start()

    def near_pass(k):
        @pl.when(a * per_dev + first != f)
        def _():
            w_pass(first, k)

    own_cum.wait()
    own_tok.wait()
    for p, d in ((0, 2), (1, 4), (1, 2), (0, 4), (0, 1), (1, 1)):
        tok_start(0, p, d)
    for r in range(1, CUBE):
        cum_copy(r).start()

    tok_wait(2, 0)
    tok_start(2, 0, 4)
    tok_start(2, 0, 1)
    tok_wait(4, 1)
    tok_start(4, 1, 2)
    tok_start(4, 1, 1)
    near_pass(0)
    near_pass(1)
    tok_wait(2, 1)
    tok_start(2, 1, 1)
    tok_wait(4, 0)
    tok_start(4, 0, 1)
    near_pass(2)
    near_pass(3)
    tok_wait(6, 0)
    tok_start(6, 0, 1)
    tok_wait(6, 1)
    tok_start(6, 1, 1)
    for r in (1, 3, 5, 7):
        for p in (0, 1):
            tok_wait(r, p)
    for r in range(1, CUBE):
        pltpu.make_async_remote_copy(
            src_ref=cums.at[c],
            dst_ref=cums.at[flip(c, r)],
            send_sem=cum_send.at[r],
            recv_sem=cum_recv.at[r],
            device_id={"ctx": flip(c, r)},
            device_id_type=MESH,
        ).wait_recv()

    def head_of(cc, i):
        return (cc % groups * per_dev + i) * shard_heads + cc // groups

    def columns(cc, i):
        return pl.ds(pl.multiple_of(head_of(cc, i) * hd, hd), hd)

    def out_copy(i, b):
        return pltpu.make_async_remote_copy(
            src_ref=stage.at[i, b],
            dst_ref=gat.at[:, columns(c, i)],
            send_sem=out_send.at[i, b],
            recv_sem=out_recv.at[i, c],
            device_id={"ctx": b},
            device_id_type=MESH,
        )

    t_pos = lax.broadcasted_iota(jnp.int32, (rows, rows), 0)
    u_pos = lax.broadcasted_iota(jnp.int32, (rows, rows), 1)

    def one(t, _):
        b = t % CUBE
        turn = t // CUBE
        i = first + (1 - 2 * first) * turn
        far = 1 - first

        @pl.when(t < CHUNKS)
        def _():
            w_pass(far, t)

        @pl.when(b == 0)
        def _():
            state[...] = jnp.zeros_like(state)

        proj = jnp.dot(tok[b], w[i], preferred_element_type=F32)
        q = jax.nn.silu(proj[:, :hd]).astype(BF16)
        k = jax.nn.silu(proj[:, hd : 2 * hd]).astype(BF16)
        v = proj[:, 2 * hd :].astype(BF16)
        row = cums[b, pl.ds(head_of(c, i), 1), :]
        col = jnp.sum(jnp.where(t_pos == u_pos, row, 0.0), axis=1, keepdims=True)
        total = row[:, rows - 1 :]
        factors = jnp.exp(jnp.where(t_pos >= u_pos, col - row, -jnp.inf))
        scores = lax.dot_general(q, k, (((1,), (1,)), ((), ())), preferred_element_type=F32)
        weights = (scores * factors).astype(BF16)
        inside = jnp.dot(weights, v, preferred_element_type=F32)
        held = state[...]
        incoming = jnp.dot(q, held.astype(BF16), preferred_element_type=F32) * jnp.exp(col)
        scaled = (k.astype(F32) * jnp.exp(total - col)).astype(BF16)
        local = lax.dot_general(scaled, v, (((0,), (0,)), ((), ())), preferred_element_type=F32)
        state[...] = jnp.exp(total) * held + local
        attended = (inside + incoming).astype(BF16)
        stage[i, b] = attended

        @pl.when(b == c)
        def _():
            gat[:, columns(c, i)] = attended

        @pl.when(b != c)
        def _():
            out_copy(i, b).start()

        return 0

    lax.fori_loop(0, per_dev * CUBE, one, 0)

    for copy in sent:
        copy.wait_send()
    for r in range(1, CUBE):
        cum_copy(r).wait_send()
    for i in range(per_dev):
        for k in range(CHUNKS):

            @pl.when(goes_up(i))
            def _():
                w_copy(i, k, True).wait_send()

            @pl.when(goes_down(i))
            def _():
                w_copy(i, k, False).wait_send()

    for i in range(per_dev):
        for r in range(1, CUBE):
            peer = flip(c, r)
            pltpu.make_async_remote_copy(
                src_ref=stage.at[i, peer],
                dst_ref=gat.at[:, columns(peer, i)],
                send_sem=out_send.at[i, peer],
                recv_sem=out_recv.at[i, peer],
                device_id={"ctx": peer},
                device_id_type=MESH,
            ).wait()

    band = 32

    def norm(n, _):
        at = pl.ds(pl.multiple_of(n * band, band), band)
        x = gat[at, :].astype(F32)
        mean_sq = jnp.sum(x * x, axis=1, keepdims=True) / feats
        out_ref[at, :] = (x * lax.rsqrt(mean_sq + 1e-05) * gain_ref[...]).astype(BF16)
        return 0

    lax.fori_loop(0, rows // band, norm, 0)


def head_body(n_ctx, n_fsdp, tokens, qkv_weight, log_decay, norm_gain):
    rows, depth = tokens.shape[1:]
    heads = log_decay.shape[1]
    feats = norm_gain.shape[0]
    hd = feats // heads
    per_dev = heads // n_ctx
    cumulative = jnp.cumsum(log_decay[0], axis=1)
    dims = (n_fsdp, heads // n_fsdp, per_dev, hd, feats)
    dma = pltpu.SemaphoreType.DMA
    vmem = pl.BlockSpec(memory_space=pltpu.VMEM)
    hbm = pl.BlockSpec(memory_space=pl.ANY)
    normed = pl.pallas_call(
        functools.partial(head_kernel, dims),
        out_shape=jax.ShapeDtypeStruct((rows, feats), BF16),
        in_specs=[hbm, hbm, vmem, vmem],
        out_specs=vmem,
        scratch_shapes=[
            pltpu.VMEM((n_ctx, rows, depth), BF16),
            pltpu.VMEM((per_dev, depth, 3 * hd), BF16),
            pltpu.VMEM((n_ctx, heads, rows), F32),
            pltpu.VMEM((per_dev, n_ctx, rows, hd), BF16),
            pltpu.VMEM((rows, feats), BF16),
            pltpu.VMEM((hd, hd), F32),
            dma((5,)),
            dma((CUBE, 2, 3)),
            dma((CUBE, 2)),
            dma((per_dev, CHUNKS)),
            dma((per_dev, CHUNKS)),
            dma((per_dev, CHUNKS)),
            dma((CUBE,)),
            dma((CUBE,)),
            dma((per_dev, n_ctx)),
            dma((per_dev, n_ctx)),
        ],
        compiler_params=pltpu.CompilerParams(
            collective_id=0, has_side_effects=True, vmem_limit_bytes=56 * 1024 * 1024
        ),
        cost_estimate=pl.CostEstimate(
            flops=6 * rows * depth * feats, bytes_accessed=16 * rows * feats, transcendentals=0
        ),
    )(tokens[0], qkv_weight, cumulative, norm_gain[None])
    return normed[None]


def entering(part, axis, combine, identity):
    place = lax.axis_index(axis)
    gathered = jax.tree.map(lambda a: lax.all_gather(a, axis), part)
    state = jax.tree.map(lambda a, e: jnp.zeros_like(a) + jnp.asarray(e, a.dtype), part, identity)

    def one(turn, state):
        return combine(
            state, jax.tree.map(lambda a: lax.dynamic_index_in_dim(a, turn, 0, False), gathered)
        )

    return lax.fori_loop(0, place, one, state)


def chain_states(decay_total, local):

    def combine(earlier, later):
        return (earlier[0] * later[0], later[0][:, None, None] * earlier[1] + later[1])

    identity_pair = (jnp.ones_like(decay_total), jnp.zeros_like(local))
    return entering((decay_total, local), "ctx", combine, identity_pair)[1]


def segment_memory_matrix(keys, values, cumulative):
    tail = jnp.exp(cumulative[:, -1:] - cumulative)
    weighted_key_vectors = (keys.astype(jnp.float32) * tail.T[:, :, None]).astype(jnp.bfloat16)
    local = jnp.einsum(
        "thd,the->hde", weighted_key_vectors, values, preferred_element_type=jnp.float32
    )
    return (jnp.exp(cumulative[:, -1]), local)


def body(tokens, qkv_weight, log_decay, norm_gain):
    inputs = tokens[0]
    log_rates = log_decay[0]
    head_count = log_rates.shape[0]
    span_len = log_rates.shape[1]
    feat_total = norm_gain.shape[0]
    head_dimension = feat_total // head_count

    def project(piece):
        return jnp.einsum("td,cde->cte", inputs, piece, preferred_element_type=jnp.float32)

    cumulative = jnp.cumsum(log_rates, axis=1)
    paired = project(lax.all_gather(qkv_weight[1:], "fsdp", axis=2, tiled=True))
    keys = jax.nn.silu(paired[0]).astype(jnp.bfloat16).reshape(span_len, head_count, head_dimension)
    values = paired[1].astype(jnp.bfloat16).reshape(span_len, head_count, head_dimension)
    decay_total, local = segment_memory_matrix(keys, values, cumulative)
    carried = chain_states(decay_total, local)
    asked = project(lax.all_gather(qkv_weight[:1], "fsdp", axis=2, tiled=True))
    queries = (
        jax.nn.silu(asked[0]).astype(jnp.bfloat16).reshape(span_len, head_count, head_dimension)
    )
    log_gaps = cumulative[:, :, None] - cumulative[:, None, :]
    causal = jnp.arange(span_len)[:, None] >= jnp.arange(span_len)[None, :]
    factors = jnp.exp(jnp.where(causal[None], log_gaps, -jnp.inf))
    scores = jnp.einsum("thd,shd->hts", queries, keys, preferred_element_type=jnp.float32)
    weights = (scores * factors).astype(jnp.bfloat16)
    inside = jnp.einsum("hts,shd->thd", weights, values, preferred_element_type=jnp.float32)
    reduced_precision_memory = carried.astype(jnp.bfloat16)
    incoming = jnp.einsum(
        "thd,hde->the", queries, reduced_precision_memory, preferred_element_type=jnp.float32
    )
    incoming = incoming * jnp.exp(cumulative).T[:, :, None]
    attention_output = (inside + incoming).reshape(span_len, feat_total)
    mean_sq = jnp.mean(attention_output * attention_output, axis=-1, keepdims=True)
    normed = (attention_output * lax.rsqrt(mean_sq + 1e-05) * norm_gain).astype(jnp.bfloat16)
    return normed[None]


def solution(mesh):
    placed = (P("fsdp", "ctx", None), P(None, None, "fsdp"), P("fsdp", None, "ctx"), P())
    n_ctx, n_fsdp = mesh.shape["ctx"], mesh.shape["fsdp"]

    def run(tokens, qkv_weight, log_decay, norm_gain):
        heads = log_decay.shape[1]
        by_head = n_ctx == CUBE and heads == 2 * n_ctx and n_fsdp % 2 == 0 and heads % n_fsdp == 0
        chosen = functools.partial(head_body, n_ctx, n_fsdp) if by_head else body
        return chosen(tokens, qkv_weight, log_decay, norm_gain)

    return jax.shard_map(
        run, mesh=mesh, in_specs=placed, out_specs=P("fsdp", "ctx", None), check_vma=False
    )
```

```python
import functools
import jax
import jax.numpy as jnp
from jax import lax
from jax.experimental import pallas as pl
from jax.experimental.pallas import tpu as pltpu
from jax.sharding import PartitionSpec as P

MESH = pl.DeviceIdType.MESH
CUBE = 8
CHUNKS = 8
F32 = jnp.float32
BF16 = jnp.bfloat16


def flip(c, r):
    out = c
    bit = 1
    while bit < CUBE:
        if r & bit:
            out = out + bit - 2 * bit * ((c // bit) % 2)
        bit *= 2
    return out


def head_kernel(
    dims,
    tok_in,
    w_in,
    cum_in,
    gain_ref,
    out_ref,
    tok,
    w,
    cums,
    stage,
    gat,
    state,
    qkv,
    local_sem,
    tok_send,
    tok_recv,
    w_up,
    w_down,
    w_recv,
    cum_send,
    cum_recv,
    out_send,
    out_recv,
):
    n_fsdp, shard_heads, per_dev, hd, feats = dims
    groups = n_fsdp // per_dev
    c = lax.axis_index("ctx")
    f = lax.axis_index("fsdp")
    j, a = c // groups, c % groups
    rows = tok.shape[1]
    half = rows // 2
    depth = w.shape[1]
    step = depth // CHUNKS

    first = jnp.where(f > a * per_dev, 1, 0)

    own_tok = pltpu.make_async_copy(tok_in, tok.at[c], local_sem.at[0])
    own_tok.start()
    own_cum = pltpu.make_async_copy(cum_in, cums.at[c], local_sem.at[1])
    own_cum.start()
    owner = f // per_dev == a
    own_i = f % per_dev

    def own_weight(p):
        return pltpu.make_async_copy(
            w_in.at[p, :, pl.ds(pl.multiple_of(j * hd, hd), hd)],
            w.at[own_i, :, pl.ds(p * hd, hd)],
            local_sem.at[2 + p],
        )

    @pl.when(owner)
    def _():
        for p in range(3):
            own_weight(p).start()

    barrier = pltpu.get_barrier_semaphore()
    for r in range(1, CUBE):
        pl.semaphore_signal(barrier, inc=1, device_id={"ctx": flip(c, r)}, device_id_type=MESH)

    @pl.when(f > 0)
    def _():
        pl.semaphore_signal(barrier, inc=1, device_id={"fsdp": f - 1}, device_id_type=MESH)

    @pl.when(f < n_fsdp - 1)
    def _():
        pl.semaphore_signal(barrier, inc=1, device_id={"fsdp": f + 1}, device_id_type=MESH)

    ends = jnp.where(f > 0, 1, 0) + jnp.where(f < n_fsdp - 1, 1, 0)
    pl.semaphore_wait(barrier, CUBE - 1 + ends)

    def tok_copy(r, p, d):
        part = tok.at[flip(c, r), pl.ds(p * half, half), :]
        return pltpu.make_async_remote_copy(
            src_ref=part,
            dst_ref=part,
            send_sem=tok_send.at[r, p, (1, 2, 4).index(d)],
            recv_sem=tok_recv.at[r ^ d, p],
            device_id={"ctx": flip(c, d)},
            device_id_type=MESH,
        )

    def tok_wait(r, p):
        part = tok.at[flip(c, r), pl.ds(p * half, half), :]
        pltpu.make_async_remote_copy(
            src_ref=part,
            dst_ref=part,
            send_sem=tok_send.at[r, p, 0],
            recv_sem=tok_recv.at[r, p],
            device_id={"ctx": flip(c, 1)},
            device_id_type=MESH,
        ).wait_recv()

    sent = []

    def tok_start(r, p, d):
        copy = tok_copy(r, p, d)
        copy.start()
        sent.append(copy)

    def w_copy(i, k, up):
        part = w.at[i, pl.ds(pl.multiple_of(k * step, step), step), :]
        return pltpu.make_async_remote_copy(
            src_ref=part,
            dst_ref=part,
            send_sem=(w_up if up else w_down).at[i, k],
            recv_sem=w_recv.at[i, k],
            device_id={"fsdp": f + 1 if up else f - 1},
            device_id_type=MESH,
        )

    def goes_up(i):
        return jnp.logical_and(a * per_dev + i <= f, f < n_fsdp - 1)

    def goes_down(i):
        return jnp.logical_and(a * per_dev + i >= f, f > 0)

    def w_pass(i, k):
        @pl.when(a * per_dev + i < f)
        def _():
            w_copy(i, k, False).wait_recv()

        @pl.when(a * per_dev + i > f)
        def _():
            w_copy(i, k, True).wait_recv()

        @pl.when(goes_up(i))
        def _():
            w_copy(i, k, True).start()

        @pl.when(goes_down(i))
        def _():
            w_copy(i, k, False).start()

    def cum_copy(r):
        return pltpu.make_async_remote_copy(
            src_ref=cums.at[c],
            dst_ref=cums.at[c],
            send_sem=cum_send.at[r],
            recv_sem=cum_recv.at[r],
            device_id={"ctx": flip(c, r)},
            device_id_type=MESH,
        )

    @pl.when(owner)
    def _():
        for p in range(3):
            own_weight(p).wait()
        for k in range(CHUNKS):

            @pl.when(f < n_fsdp - 1)
            def _():
                w_copy(own_i, k, True).start()

            @pl.when(f > 0)
            def _():
                w_copy(own_i, k, False).start()

    inner = jnp.logical_and(f > 0, f < n_fsdp - 1)

    def inner_pass(i, ks):
        @pl.when(jnp.logical_and(inner, a * per_dev + i != f))
        def _():
            for k in ks:
                w_pass(i, k)

    def end_wait(i):
        @pl.when(jnp.logical_and(f == 0, a * per_dev + i > f))
        def _():
            for k in range(CHUNKS):
                w_copy(i, k, True).wait_recv()

        @pl.when(jnp.logical_and(f == n_fsdp - 1, a * per_dev + i < f))
        def _():
            for k in range(CHUNKS):
                w_copy(i, k, False).wait_recv()

    far = 1 - first
    early, late = range(CHUNKS // 2), range(CHUNKS // 2, CHUNKS)
    own_cum.wait()
    own_tok.wait()
    for p, d in ((0, 2), (1, 4), (1, 2), (0, 4), (0, 1), (1, 1)):
        tok_start(0, p, d)
    for r in range(1, CUBE):
        cum_copy(r).start()

    inner_pass(first, early)
    tok_wait(2, 0)
    tok_start(2, 0, 4)
    tok_start(2, 0, 1)
    tok_wait(4, 1)
    tok_start(4, 1, 2)
    tok_start(4, 1, 1)
    inner_pass(first, late)
    inner_pass(far, early)
    tok_wait(2, 1)
    tok_start(2, 1, 1)
    tok_wait(4, 0)
    tok_start(4, 0, 1)
    inner_pass(far, late)
    tok_wait(6, 0)
    tok_start(6, 0, 1)
    tok_wait(6, 1)
    tok_start(6, 1, 1)
    end_wait(first)
    for r in (1, 3, 5, 7):
        for p in (0, 1):
            tok_wait(r, p)
    for r in range(1, CUBE):
        pltpu.make_async_remote_copy(
            src_ref=cums.at[c],
            dst_ref=cums.at[flip(c, r)],
            send_sem=cum_send.at[r],
            recv_sem=cum_recv.at[r],
            device_id={"ctx": flip(c, r)},
            device_id_type=MESH,
        ).wait_recv()

    def head_of(cc, i):
        return (cc % groups * per_dev + i) * shard_heads + cc // groups

    def columns(cc, i):
        return pl.ds(pl.multiple_of(head_of(cc, i) * hd, hd), hd)

    def out_copy(i, b):
        return pltpu.make_async_remote_copy(
            src_ref=stage.at[i, b],
            dst_ref=gat.at[:, columns(c, i)],
            send_sem=out_send.at[i, b],
            recv_sem=out_recv.at[i, c],
            device_id={"ctx": b},
            device_id_type=MESH,
        )

    t_pos = lax.broadcasted_iota(jnp.int32, (rows, rows), 0)
    u_pos = lax.broadcasted_iota(jnp.int32, (rows, rows), 1)

    def place(t):
        turn = t // CUBE
        return first + (1 - 2 * first) * turn, t % CUBE

    def project(t):
        i, b = place(t)
        return jnp.dot(tok[b], w[i], preferred_element_type=F32)

    def keep(t, proj):
        qkv[t % 2, :, : 2 * hd] = jax.nn.silu(proj[:, : 2 * hd]).astype(BF16)
        qkv[t % 2, :, 2 * hd :] = proj[:, 2 * hd :].astype(BF16)

    def attend(t, ahead):
        i, b = place(t)

        @pl.when(b == 0)
        def _():
            state[...] = jnp.zeros_like(state)

        q = qkv[t % 2, :, :hd]
        k = qkv[t % 2, :, hd : 2 * hd]
        v = qkv[t % 2, :, 2 * hd :]
        row = cums[b, pl.ds(head_of(c, i), 1), :]
        held = state[...]
        proj = project(t + 1) if ahead else None
        col = jnp.sum(jnp.where(t_pos == u_pos, row, 0.0), axis=1, keepdims=True)
        total = row[:, rows - 1 :]
        factors = jnp.exp(jnp.where(t_pos >= u_pos, col - row, -jnp.inf))
        scores = lax.dot_general(q, k, (((1,), (1,)), ((), ())), preferred_element_type=F32)
        weights = (scores * factors).astype(BF16)
        inside = jnp.dot(weights, v, preferred_element_type=F32)
        incoming = jnp.dot(q, held.astype(BF16), preferred_element_type=F32) * jnp.exp(col)
        scaled = (k.astype(F32) * jnp.exp(total - col)).astype(BF16)
        local = lax.dot_general(scaled, v, (((0,), (0,)), ((), ())), preferred_element_type=F32)
        state[...] = jnp.exp(total) * held + local
        attended = (inside + incoming).astype(BF16)
        stage[i, b] = attended
        if ahead:
            keep(t + 1, proj)

        @pl.when(b == c)
        def _():
            gat[:, columns(c, i)] = stage[i, b]

        @pl.when(b != c)
        def _():
            out_copy(i, b).start()

    def one(t, _):
        @pl.when(t == CUBE - 1)
        def _():
            end_wait(far)

        attend(t, True)
        return 0

    keep(0, project(0))
    lax.fori_loop(0, per_dev * CUBE - 1, one, 0)
    attend(per_dev * CUBE - 1, False)

    for copy in sent:
        copy.wait_send()
    for r in range(1, CUBE):
        cum_copy(r).wait_send()
    for i in range(per_dev):
        for k in range(CHUNKS):

            @pl.when(goes_up(i))
            def _():
                w_copy(i, k, True).wait_send()

            @pl.when(goes_down(i))
            def _():
                w_copy(i, k, False).wait_send()

    for i in range(per_dev):
        for r in range(1, CUBE):
            peer = flip(c, r)
            pltpu.make_async_remote_copy(
                src_ref=stage.at[i, peer],
                dst_ref=gat.at[:, columns(peer, i)],
                send_sem=out_send.at[i, peer],
                recv_sem=out_recv.at[i, peer],
                device_id={"ctx": peer},
                device_id_type=MESH,
            ).wait()

    band = 32

    def norm(n, _):
        at = pl.ds(pl.multiple_of(n * band, band), band)
        x = gat[at, :].astype(F32)
        mean_sq = jnp.sum(x * x, axis=1, keepdims=True) / feats
        out_ref[at, :] = (x * lax.rsqrt(mean_sq + 1e-05) * gain_ref[...]).astype(BF16)
        return 0

    lax.fori_loop(0, rows // band, norm, 0)


def head_body(n_ctx, n_fsdp, tokens, qkv_weight, log_decay, norm_gain):
    rows, depth = tokens.shape[1:]
    heads = log_decay.shape[1]
    feats = norm_gain.shape[0]
    hd = feats // heads
    per_dev = heads // n_ctx
    cumulative = jnp.cumsum(log_decay[0], axis=1)
    dims = (n_fsdp, heads // n_fsdp, per_dev, hd, feats)
    dma = pltpu.SemaphoreType.DMA
    vmem = pl.BlockSpec(memory_space=pltpu.VMEM)
    hbm = pl.BlockSpec(memory_space=pl.ANY)
    normed = pl.pallas_call(
        functools.partial(head_kernel, dims),
        out_shape=jax.ShapeDtypeStruct((rows, feats), BF16),
        in_specs=[hbm, hbm, vmem, vmem],
        out_specs=vmem,
        scratch_shapes=[
            pltpu.VMEM((n_ctx, rows, depth), BF16),
            pltpu.VMEM((per_dev, depth, 3 * hd), BF16),
            pltpu.VMEM((n_ctx, heads, rows), F32),
            pltpu.VMEM((per_dev, n_ctx, rows, hd), BF16),
            pltpu.VMEM((rows, feats), BF16),
            pltpu.VMEM((hd, hd), F32),
            pltpu.VMEM((2, rows, 3 * hd), BF16),
            dma((5,)),
            dma((CUBE, 2, 3)),
            dma((CUBE, 2)),
            dma((per_dev, CHUNKS)),
            dma((per_dev, CHUNKS)),
            dma((per_dev, CHUNKS)),
            dma((CUBE,)),
            dma((CUBE,)),
            dma((per_dev, n_ctx)),
            dma((per_dev, n_ctx)),
        ],
        compiler_params=pltpu.CompilerParams(
            collective_id=0, has_side_effects=True, vmem_limit_bytes=56 * 1024 * 1024
        ),
        cost_estimate=pl.CostEstimate(
            flops=6 * rows * depth * feats, bytes_accessed=16 * rows * feats, transcendentals=0
        ),
    )(tokens[0], qkv_weight, cumulative, norm_gain[None])
    return normed[None]


def entering(part, axis, combine, identity):
    place = lax.axis_index(axis)
    gathered = jax.tree.map(lambda a: lax.all_gather(a, axis), part)
    state = jax.tree.map(lambda a, e: jnp.zeros_like(a) + jnp.asarray(e, a.dtype), part, identity)

    def one(turn, state):
        return combine(
            state, jax.tree.map(lambda a: lax.dynamic_index_in_dim(a, turn, 0, False), gathered)
        )

    return lax.fori_loop(0, place, one, state)


def chain_states(decay_total, local):

    def combine(earlier, later):
        return (earlier[0] * later[0], later[0][:, None, None] * earlier[1] + later[1])

    identity_pair = (jnp.ones_like(decay_total), jnp.zeros_like(local))
    return entering((decay_total, local), "ctx", combine, identity_pair)[1]


def segment_memory_matrix(keys, values, cumulative):
    tail = jnp.exp(cumulative[:, -1:] - cumulative)
    weighted_key_vectors = (keys.astype(jnp.float32) * tail.T[:, :, None]).astype(jnp.bfloat16)
    local = jnp.einsum(
        "thd,the->hde", weighted_key_vectors, values, preferred_element_type=jnp.float32
    )
    return (jnp.exp(cumulative[:, -1]), local)


def body(tokens, qkv_weight, log_decay, norm_gain):
    inputs = tokens[0]
    log_rates = log_decay[0]
    head_count = log_rates.shape[0]
    span_len = log_rates.shape[1]
    feat_total = norm_gain.shape[0]
    head_dimension = feat_total // head_count

    def project(piece):
        return jnp.einsum("td,cde->cte", inputs, piece, preferred_element_type=jnp.float32)

    cumulative = jnp.cumsum(log_rates, axis=1)
    paired = project(lax.all_gather(qkv_weight[1:], "fsdp", axis=2, tiled=True))
    keys = jax.nn.silu(paired[0]).astype(jnp.bfloat16).reshape(span_len, head_count, head_dimension)
    values = paired[1].astype(jnp.bfloat16).reshape(span_len, head_count, head_dimension)
    decay_total, local = segment_memory_matrix(keys, values, cumulative)
    carried = chain_states(decay_total, local)
    asked = project(lax.all_gather(qkv_weight[:1], "fsdp", axis=2, tiled=True))
    queries = (
        jax.nn.silu(asked[0]).astype(jnp.bfloat16).reshape(span_len, head_count, head_dimension)
    )
    log_gaps = cumulative[:, :, None] - cumulative[:, None, :]
    causal = jnp.arange(span_len)[:, None] >= jnp.arange(span_len)[None, :]
    factors = jnp.exp(jnp.where(causal[None], log_gaps, -jnp.inf))
    scores = jnp.einsum("thd,shd->hts", queries, keys, preferred_element_type=jnp.float32)
    weights = (scores * factors).astype(jnp.bfloat16)
    inside = jnp.einsum("hts,shd->thd", weights, values, preferred_element_type=jnp.float32)
    reduced_precision_memory = carried.astype(jnp.bfloat16)
    incoming = jnp.einsum(
        "thd,hde->the", queries, reduced_precision_memory, preferred_element_type=jnp.float32
    )
    incoming = incoming * jnp.exp(cumulative).T[:, :, None]
    attention_output = (inside + incoming).reshape(span_len, feat_total)
    mean_sq = jnp.mean(attention_output * attention_output, axis=-1, keepdims=True)
    normed = (attention_output * lax.rsqrt(mean_sq + 1e-05) * norm_gain).astype(jnp.bfloat16)
    return normed[None]


def solution(mesh):
    placed = (P("fsdp", "ctx", None), P(None, None, "fsdp"), P("fsdp", None, "ctx"), P())
    n_ctx, n_fsdp = mesh.shape["ctx"], mesh.shape["fsdp"]

    def run(tokens, qkv_weight, log_decay, norm_gain):
        heads = log_decay.shape[1]
        by_head = n_ctx == CUBE and heads == 2 * n_ctx and n_fsdp % 2 == 0 and heads % n_fsdp == 0
        chosen = functools.partial(head_body, n_ctx, n_fsdp) if by_head else body
        return chosen(tokens, qkv_weight, log_decay, norm_gain)

    return jax.shard_map(
        run, mesh=mesh, in_specs=placed, out_specs=P("fsdp", "ctx", None), check_vma=False
    )
```

```python
import functools
import jax
import jax.numpy as jnp
from jax import lax
from jax.experimental import pallas as pl
from jax.experimental.pallas import tpu as pltpu
from jax.sharding import PartitionSpec as P

MESH = pl.DeviceIdType.MESH
CUBE = 8
CHUNKS = 8
F32 = jnp.float32
BF16 = jnp.bfloat16


def flip(c, r):
    out = c
    bit = 1
    while bit < CUBE:
        if r & bit:
            out = out + bit - 2 * bit * ((c // bit) % 2)
        bit *= 2
    return out


def head_kernel(
    dims,
    tok_in,
    w_in,
    decay_in,
    gain_ref,
    out_ref,
    tok,
    w,
    cums,
    stage,
    gat,
    state,
    sums,
    factors,
    opening,
    closing,
    near_qkv,
    far_qkv,
    partial,
    local_sem,
    tok_send,
    tok_recv,
    w_up,
    w_down,
    w_recv,
    cum_send,
    cum_recv,
    out_send,
    out_recv,
):
    n_fsdp, shard_heads, per_dev, hd, feats = dims
    groups = n_fsdp // per_dev
    c = lax.axis_index("ctx")
    f = lax.axis_index("fsdp")
    j, a = c // groups, c % groups
    rows = tok.shape[1]
    half = rows // 2
    depth = w.shape[1]
    step = depth // CHUNKS

    first = jnp.where(f > a * per_dev, 1, 0)

    own_tok = pltpu.make_async_copy(tok_in.at[0], tok.at[c], local_sem.at[0])
    own_tok.start()
    cums[c] = decay_in[0]
    owner = f // per_dev == a
    own_i = f % per_dev

    def own_weight(p):
        return pltpu.make_async_copy(
            w_in.at[p, :, pl.ds(pl.multiple_of(j * hd, hd), hd)],
            w.at[own_i, :, pl.ds(p * hd, hd)],
            local_sem.at[1 + p],
        )

    @pl.when(owner)
    def _():
        for p in range(3):
            own_weight(p).start()

    barrier = pltpu.get_barrier_semaphore()
    for r in range(1, CUBE):
        pl.semaphore_signal(barrier, inc=1, device_id={"ctx": flip(c, r)}, device_id_type=MESH)

    @pl.when(f > 0)
    def _():
        pl.semaphore_signal(barrier, inc=1, device_id={"fsdp": f - 1}, device_id_type=MESH)

    @pl.when(f < n_fsdp - 1)
    def _():
        pl.semaphore_signal(barrier, inc=1, device_id={"fsdp": f + 1}, device_id_type=MESH)

    ends = jnp.where(f > 0, 1, 0) + jnp.where(f < n_fsdp - 1, 1, 0)
    pl.semaphore_wait(barrier, CUBE - 1 + ends)

    def tok_copy(r, p, d):
        part = tok.at[flip(c, r), pl.ds(p * half, half), :]
        return pltpu.make_async_remote_copy(
            src_ref=part,
            dst_ref=part,
            send_sem=tok_send.at[r, p, (1, 2, 4).index(d)],
            recv_sem=tok_recv.at[r ^ d, p],
            device_id={"ctx": flip(c, d)},
            device_id_type=MESH,
        )

    def tok_wait(r, p):
        part = tok.at[flip(c, r), pl.ds(p * half, half), :]
        pltpu.make_async_remote_copy(
            src_ref=part,
            dst_ref=part,
            send_sem=tok_send.at[r, p, 0],
            recv_sem=tok_recv.at[r, p],
            device_id={"ctx": flip(c, 1)},
            device_id_type=MESH,
        ).wait_recv()

    sent = []

    def tok_start(r, p, d):
        copy = tok_copy(r, p, d)
        copy.start()
        sent.append(copy)

    def w_copy(i, k, up):
        part = w.at[i, pl.ds(pl.multiple_of(k * step, step), step), :]
        return pltpu.make_async_remote_copy(
            src_ref=part,
            dst_ref=part,
            send_sem=(w_up if up else w_down).at[i, k],
            recv_sem=w_recv.at[i, k],
            device_id={"fsdp": f + 1 if up else f - 1},
            device_id_type=MESH,
        )

    def goes_up(i):
        return jnp.logical_and(a * per_dev + i <= f, f < n_fsdp - 1)

    def goes_down(i):
        return jnp.logical_and(a * per_dev + i >= f, f > 0)

    def w_pass(i, k):
        @pl.when(a * per_dev + i < f)
        def _():
            w_copy(i, k, False).wait_recv()

        @pl.when(a * per_dev + i > f)
        def _():
            w_copy(i, k, True).wait_recv()

        @pl.when(goes_up(i))
        def _():
            w_copy(i, k, True).start()

        @pl.when(goes_down(i))
        def _():
            w_copy(i, k, False).start()

    def cum_copy(r):
        return pltpu.make_async_remote_copy(
            src_ref=decay_in.at[0],
            dst_ref=cums.at[c],
            send_sem=cum_send.at[r],
            recv_sem=cum_recv.at[r],
            device_id={"ctx": flip(c, r)},
            device_id_type=MESH,
        )

    for r in range(1, CUBE):
        cum_copy(r).start()

    own_tok.wait()
    for p, d in ((0, 2), (1, 4), (1, 2), (0, 4), (0, 1), (1, 1)):
        tok_start(0, p, d)

    @pl.when(owner)
    def _():
        for p in range(3):
            own_weight(p).wait()
        for k in range(CHUNKS):

            @pl.when(f < n_fsdp - 1)
            def _():
                w_copy(own_i, k, True).start()

            @pl.when(f > 0)
            def _():
                w_copy(own_i, k, False).start()

    inner = jnp.logical_and(f > 0, f < n_fsdp - 1)

    def inner_pass(i, ks):
        @pl.when(jnp.logical_and(inner, a * per_dev + i != f))
        def _():
            for k in ks:
                w_pass(i, k)

    def end_wait(i, ks):
        @pl.when(jnp.logical_and(f == 0, a * per_dev + i > f))
        def _():
            for k in ks:
                w_copy(i, k, True).wait_recv()

        @pl.when(jnp.logical_and(f == n_fsdp - 1, a * per_dev + i < f))
        def _():
            for k in ks:
                w_copy(i, k, False).wait_recv()

    far = 1 - first
    early, late = range(CHUNKS // 2), range(CHUNKS // 2, CHUNKS)
    def head_of(cc, i):
        return (cc % groups * per_dev + i) * shard_heads + cc // groups

    def columns(cc, i):
        return pl.ds(pl.multiple_of(head_of(cc, i) * hd, hd), hd)

    def out_copy(i, b):
        return pltpu.make_async_remote_copy(
            src_ref=stage.at[i, b],
            dst_ref=gat.at[:, columns(c, i)],
            send_sem=out_send.at[i, b],
            recv_sem=out_recv.at[i, c],
            device_id={"ctx": b},
            device_id_type=MESH,
        )

    for r in range(1, CUBE):
        pltpu.make_async_remote_copy(
            src_ref=decay_in.at[0],
            dst_ref=cums.at[flip(c, r)],
            send_sem=cum_send.at[r],
            recv_sem=cum_recv.at[r],
            device_id={"ctx": flip(c, r)},
            device_id_type=MESH,
        ).wait_recv()

    t_pos = lax.broadcasted_iota(jnp.int32, (rows, rows), 0)
    u_pos = lax.broadcasted_iota(jnp.int32, (rows, rows), 1)
    upto = jnp.where(t_pos <= u_pos, 1.0, 0.0).astype(F32)
    for i in range(per_dev):
        rates = jnp.concatenate(
            [cums[b, pl.ds(head_of(c, i), 1), :] for b in range(CUBE)], axis=0
        )
        sums[i] = jnp.dot(
            rates, upto, preferred_element_type=F32, precision=lax.Precision.HIGHEST
        )

    def decays(n, _):
        i, b = n // CUBE, n % CUBE
        row = sums[i, pl.ds(b, 1), :]
        col = jnp.sum(jnp.where(t_pos == u_pos, row, 0.0), axis=1, keepdims=True)
        factors[i, b] = jnp.exp(jnp.where(t_pos >= u_pos, col - row, -jnp.inf))
        opening[i, b] = jnp.broadcast_to(jnp.exp(col), (rows, hd))
        closing[i, b] = jnp.broadcast_to(jnp.exp(row[:, rows - 1 :] - col), (rows, hd))
        return 0

    lax.fori_loop(0, per_dev * CUBE, decays, 0)

    def activate(proj):
        qk = jax.nn.silu(proj[:, : 2 * hd]).astype(BF16)
        return jnp.concatenate([qk, proj[:, 2 * hd :].astype(BF16)], axis=1)

    def near_project(r, _):
        b = c
        bit = 1
        while bit < CUBE:
            b = b + ((r // bit) % 2) * (bit - 2 * bit * ((c // bit) % 2))
            bit *= 2
        near_qkv[b] = activate(jnp.dot(tok[b], w[first], preferred_element_type=F32))
        return 0

    inner_pass(first, early)
    tok_wait(2, 0)
    tok_start(2, 0, 4)
    tok_start(2, 0, 1)
    tok_wait(4, 1)
    tok_start(4, 1, 2)
    tok_start(4, 1, 1)
    inner_pass(first, late)
    inner_pass(far, early)
    tok_wait(2, 1)
    tok_start(2, 1, 1)
    tok_wait(4, 0)
    tok_start(4, 0, 1)
    inner_pass(far, late)
    end_wait(first, range(CHUNKS))
    for r in (1, 3, 5):
        for p in (0, 1):
            tok_wait(r, p)
    lax.fori_loop(0, 6, near_project, 0)
    tok_wait(6, 0)
    tok_start(6, 0, 1)
    tok_wait(6, 1)
    tok_start(6, 1, 1)
    for p in (0, 1):
        tok_wait(7, p)
    lax.fori_loop(6, CUBE, near_project, 0)

    def attend(i, b, qkv, ahead):
        q, k, v = qkv[:, :hd], qkv[:, hd : 2 * hd], qkv[:, 2 * hd :]

        @pl.when(b == 0)
        def _():
            state[...] = jnp.zeros_like(state)

        held = state[...]
        if ahead is not None:
            ahead()
        scores = lax.dot_general(q, k, (((1,), (1,)), ((), ())), preferred_element_type=F32)
        weights = (scores * factors[i, b]).astype(BF16)
        inside = jnp.dot(weights, v, preferred_element_type=F32)
        incoming = jnp.dot(q, held.astype(BF16), preferred_element_type=F32) * opening[i, b]
        scaled = (k.astype(F32) * closing[i, b]).astype(BF16)
        local = lax.dot_general(scaled, v, (((0,), (0,)), ((), ())), preferred_element_type=F32)
        total = jnp.exp(sums[i, pl.ds(b, 1), :][:, rows - 1 :])
        state[...] = total * held + local
        stage[i, b] = (inside + incoming).astype(BF16)

        @pl.when(b == c)
        def _():
            gat[:, columns(c, i)] = stage[i, b]

        @pl.when(b != c)
        def _():
            out_copy(i, b).start()

    def near_one(b, _):
        attend(first, b, near_qkv[b], None)
        return 0

    lax.fori_loop(0, CUBE, near_one, 0)

    def piece(b, lo, hi):
        at = pl.ds(lo * step, (hi - lo) * step)
        return jnp.dot(tok[b, :, at], w[far, at, :], preferred_element_type=F32)

    half_way, most = CHUNKS // 2, CHUNKS - CHUNKS // 4

    def grow_first(b, _):
        partial[b] = piece(b, 0, half_way)
        return 0

    def grow_next(b, _):
        partial[b] += piece(b, half_way, most)
        return 0

    def finish(b):
        far_qkv[b % 2] = activate(partial[b] + piece(b, most, CHUNKS))

    end_wait(far, range(half_way))
    lax.fori_loop(0, CUBE, grow_first, 0)
    end_wait(far, range(half_way, most))
    lax.fori_loop(0, CUBE, grow_next, 0)
    end_wait(far, range(most, CHUNKS))
    finish(0)

    def far_one(b, _):
        attend(far, b, far_qkv[b % 2], functools.partial(finish, b + 1))
        return 0

    lax.fori_loop(0, CUBE - 1, far_one, 0)
    attend(far, CUBE - 1, far_qkv[(CUBE - 1) % 2], None)

    for copy in sent:
        copy.wait_send()
    for r in range(1, CUBE):
        cum_copy(r).wait_send()
    for i in range(per_dev):
        for k in range(CHUNKS):

            @pl.when(goes_up(i))
            def _():
                w_copy(i, k, True).wait_send()

            @pl.when(goes_down(i))
            def _():
                w_copy(i, k, False).wait_send()

    for i in range(per_dev):
        for r in range(1, CUBE):
            peer = flip(c, r)
            pltpu.make_async_remote_copy(
                src_ref=stage.at[i, peer],
                dst_ref=gat.at[:, columns(peer, i)],
                send_sem=out_send.at[i, peer],
                recv_sem=out_recv.at[i, peer],
                device_id={"ctx": peer},
                device_id_type=MESH,
            ).wait()

    band = 32

    def norm(n, _):
        at = pl.ds(pl.multiple_of(n * band, band), band)
        x = gat[at, :].astype(F32)
        mean_sq = jnp.sum(x * x, axis=1, keepdims=True) / feats
        out_ref[0, at, :] = (x * lax.rsqrt(mean_sq + 1e-05) * gain_ref[...]).astype(BF16)
        return 0

    lax.fori_loop(0, rows // band, norm, 0)


def head_body(n_ctx, n_fsdp, tokens, qkv_weight, log_decay, norm_gain):
    rows, depth = tokens.shape[1:]
    heads = log_decay.shape[1]
    feats = norm_gain.shape[0]
    hd = feats // heads
    per_dev = heads // n_ctx
    dims = (n_fsdp, heads // n_fsdp, per_dev, hd, feats)
    dma = pltpu.SemaphoreType.DMA
    vmem = pl.BlockSpec(memory_space=pltpu.VMEM)
    hbm = pl.BlockSpec(memory_space=pl.ANY)
    normed = pl.pallas_call(
        functools.partial(head_kernel, dims),
        out_shape=jax.ShapeDtypeStruct((1, rows, feats), BF16),
        in_specs=[hbm, hbm, vmem, vmem],
        out_specs=vmem,
        scratch_shapes=[
            pltpu.VMEM((n_ctx, rows, depth), BF16),
            pltpu.VMEM((per_dev, depth, 3 * hd), BF16),
            pltpu.VMEM((n_ctx, heads, rows), F32),
            pltpu.VMEM((per_dev, n_ctx, rows, hd), BF16),
            pltpu.VMEM((rows, feats), BF16),
            pltpu.VMEM((hd, hd), F32),
            pltpu.VMEM((per_dev, n_ctx, rows), F32),
            pltpu.VMEM((per_dev, n_ctx, rows, rows), F32),
            pltpu.VMEM((per_dev, n_ctx, rows, hd), F32),
            pltpu.VMEM((per_dev, n_ctx, rows, hd), F32),
            pltpu.VMEM((n_ctx, rows, 3 * hd), BF16),
            pltpu.VMEM((2, rows, 3 * hd), BF16),
            pltpu.VMEM((n_ctx, rows, 3 * hd), F32),
            dma((4,)),
            dma((CUBE, 2, 3)),
            dma((CUBE, 2)),
            dma((per_dev, CHUNKS)),
            dma((per_dev, CHUNKS)),
            dma((per_dev, CHUNKS)),
            dma((CUBE,)),
            dma((CUBE,)),
            dma((per_dev, n_ctx)),
            dma((per_dev, n_ctx)),
        ],
        compiler_params=pltpu.CompilerParams(
            collective_id=0, has_side_effects=True, vmem_limit_bytes=56 * 1024 * 1024
        ),
        cost_estimate=pl.CostEstimate(
            flops=6 * rows * depth * feats, bytes_accessed=16 * rows * feats, transcendentals=0
        ),
    )(tokens, qkv_weight, log_decay, norm_gain[None])
    return normed


def entering(part, axis, combine, identity):
    place = lax.axis_index(axis)
    gathered = jax.tree.map(lambda a: lax.all_gather(a, axis), part)
    state = jax.tree.map(lambda a, e: jnp.zeros_like(a) + jnp.asarray(e, a.dtype), part, identity)

    def one(turn, state):
        return combine(
            state, jax.tree.map(lambda a: lax.dynamic_index_in_dim(a, turn, 0, False), gathered)
        )

    return lax.fori_loop(0, place, one, state)


def chain_states(decay_total, local):

    def combine(earlier, later):
        return (earlier[0] * later[0], later[0][:, None, None] * earlier[1] + later[1])

    identity_pair = (jnp.ones_like(decay_total), jnp.zeros_like(local))
    return entering((decay_total, local), "ctx", combine, identity_pair)[1]


def segment_memory_matrix(keys, values, cumulative):
    tail = jnp.exp(cumulative[:, -1:] - cumulative)
    weighted_key_vectors = (keys.astype(jnp.float32) * tail.T[:, :, None]).astype(jnp.bfloat16)
    local = jnp.einsum(
        "thd,the->hde", weighted_key_vectors, values, preferred_element_type=jnp.float32
    )
    return (jnp.exp(cumulative[:, -1]), local)


def body(tokens, qkv_weight, log_decay, norm_gain):
    inputs = tokens[0]
    log_rates = log_decay[0]
    head_count = log_rates.shape[0]
    span_len = log_rates.shape[1]
    feat_total = norm_gain.shape[0]
    head_dimension = feat_total // head_count

    def project(piece):
        return jnp.einsum("td,cde->cte", inputs, piece, preferred_element_type=jnp.float32)

    cumulative = jnp.cumsum(log_rates, axis=1)
    paired = project(lax.all_gather(qkv_weight[1:], "fsdp", axis=2, tiled=True))
    keys = jax.nn.silu(paired[0]).astype(jnp.bfloat16).reshape(span_len, head_count, head_dimension)
    values = paired[1].astype(jnp.bfloat16).reshape(span_len, head_count, head_dimension)
    decay_total, local = segment_memory_matrix(keys, values, cumulative)
    carried = chain_states(decay_total, local)
    asked = project(lax.all_gather(qkv_weight[:1], "fsdp", axis=2, tiled=True))
    queries = (
        jax.nn.silu(asked[0]).astype(jnp.bfloat16).reshape(span_len, head_count, head_dimension)
    )
    log_gaps = cumulative[:, :, None] - cumulative[:, None, :]
    causal = jnp.arange(span_len)[:, None] >= jnp.arange(span_len)[None, :]
    factors = jnp.exp(jnp.where(causal[None], log_gaps, -jnp.inf))
    scores = jnp.einsum("thd,shd->hts", queries, keys, preferred_element_type=jnp.float32)
    weights = (scores * factors).astype(jnp.bfloat16)
    inside = jnp.einsum("hts,shd->thd", weights, values, preferred_element_type=jnp.float32)
    reduced_precision_memory = carried.astype(jnp.bfloat16)
    incoming = jnp.einsum(
        "thd,hde->the", queries, reduced_precision_memory, preferred_element_type=jnp.float32
    )
    incoming = incoming * jnp.exp(cumulative).T[:, :, None]
    attention_output = (inside + incoming).reshape(span_len, feat_total)
    mean_sq = jnp.mean(attention_output * attention_output, axis=-1, keepdims=True)
    normed = (attention_output * lax.rsqrt(mean_sq + 1e-05) * norm_gain).astype(jnp.bfloat16)
    return normed[None]


def solution(mesh):
    placed = (P("fsdp", "ctx", None), P(None, None, "fsdp"), P("fsdp", None, "ctx"), P())
    n_ctx, n_fsdp = mesh.shape["ctx"], mesh.shape["fsdp"]

    def run(tokens, qkv_weight, log_decay, norm_gain):
        heads = log_decay.shape[1]
        by_head = n_ctx == CUBE and heads == 2 * n_ctx and n_fsdp % 2 == 0 and heads % n_fsdp == 0
        chosen = functools.partial(head_body, n_ctx, n_fsdp) if by_head else body
        return chosen(tokens, qkv_weight, log_decay, norm_gain)

    return jax.shard_map(
        run, mesh=mesh, in_specs=placed, out_specs=P("fsdp", "ctx", None), check_vma=False
    )
```

```python
import functools
import jax
import jax.numpy as jnp
from jax import lax
from jax.experimental import pallas as pl
from jax.experimental.pallas import tpu as pltpu
from jax.sharding import PartitionSpec as P

MESH = pl.DeviceIdType.MESH
CUBE = 8
CHUNKS = 8
F32 = jnp.float32
BF16 = jnp.bfloat16


def flip(c, r):
    out = c
    bit = 1
    while bit < CUBE:
        if r & bit:
            out = out + bit - 2 * bit * ((c // bit) % 2)
        bit *= 2
    return out


def head_kernel(
    dims,
    tok_in,
    w_in,
    decay_in,
    gain_ref,
    out_ref,
    tok,
    w,
    cums,
    stage,
    gat,
    state,
    sums,
    factors,
    opening,
    closing,
    near_q,
    near_inside,
    near_local,
    far_qkv,
    partial,
    local_sem,
    tok_send,
    tok_recv,
    w_up,
    w_down,
    w_recv,
    cum_send,
    cum_recv,
    out_send,
    out_recv,
):
    n_fsdp, shard_heads, per_dev, hd, feats = dims
    groups = n_fsdp // per_dev
    c = lax.axis_index("ctx")
    f = lax.axis_index("fsdp")
    j, a = c // groups, c % groups
    rows = tok.shape[1]
    half = rows // 2
    depth = w.shape[1]
    step = depth // CHUNKS

    first = jnp.where(f > a * per_dev, 1, 0)

    own_tok = pltpu.make_async_copy(tok_in.at[0], tok.at[c], local_sem.at[0])
    own_tok.start()
    cums[c] = decay_in[0]
    owner = f // per_dev == a
    own_i = f % per_dev

    def own_weight(p):
        return pltpu.make_async_copy(
            w_in.at[p, :, pl.ds(pl.multiple_of(j * hd, hd), hd)],
            w.at[own_i, :, pl.ds(p * hd, hd)],
            local_sem.at[1 + p],
        )

    @pl.when(owner)
    def _():
        for p in range(3):
            own_weight(p).start()

    barrier = pltpu.get_barrier_semaphore()
    for r in range(1, CUBE):
        pl.semaphore_signal(barrier, inc=1, device_id={"ctx": flip(c, r)}, device_id_type=MESH)

    @pl.when(f > 0)
    def _():
        pl.semaphore_signal(barrier, inc=1, device_id={"fsdp": f - 1}, device_id_type=MESH)

    @pl.when(f < n_fsdp - 1)
    def _():
        pl.semaphore_signal(barrier, inc=1, device_id={"fsdp": f + 1}, device_id_type=MESH)

    ends = jnp.where(f > 0, 1, 0) + jnp.where(f < n_fsdp - 1, 1, 0)
    pl.semaphore_wait(barrier, CUBE - 1 + ends)

    def tok_copy(r, p, d):
        part = tok.at[flip(c, r), pl.ds(p * half, half), :]
        return pltpu.make_async_remote_copy(
            src_ref=part,
            dst_ref=part,
            send_sem=tok_send.at[r, p, (1, 2, 4).index(d)],
            recv_sem=tok_recv.at[r ^ d, p],
            device_id={"ctx": flip(c, d)},
            device_id_type=MESH,
        )

    def tok_wait(r, p):
        part = tok.at[flip(c, r), pl.ds(p * half, half), :]
        pltpu.make_async_remote_copy(
            src_ref=part,
            dst_ref=part,
            send_sem=tok_send.at[r, p, 0],
            recv_sem=tok_recv.at[r, p],
            device_id={"ctx": flip(c, 1)},
            device_id_type=MESH,
        ).wait_recv()

    sent = []

    def tok_start(r, p, d):
        copy = tok_copy(r, p, d)
        copy.start()
        sent.append(copy)

    def w_copy(i, k, up):
        part = w.at[i, pl.ds(pl.multiple_of(k * step, step), step), :]
        return pltpu.make_async_remote_copy(
            src_ref=part,
            dst_ref=part,
            send_sem=(w_up if up else w_down).at[i, k],
            recv_sem=w_recv.at[i, k],
            device_id={"fsdp": f + 1 if up else f - 1},
            device_id_type=MESH,
        )

    def goes_up(i):
        return jnp.logical_and(a * per_dev + i <= f, f < n_fsdp - 1)

    def goes_down(i):
        return jnp.logical_and(a * per_dev + i >= f, f > 0)

    def w_pass(i, k):
        @pl.when(a * per_dev + i < f)
        def _():
            w_copy(i, k, False).wait_recv()

        @pl.when(a * per_dev + i > f)
        def _():
            w_copy(i, k, True).wait_recv()

        @pl.when(goes_up(i))
        def _():
            w_copy(i, k, True).start()

        @pl.when(goes_down(i))
        def _():
            w_copy(i, k, False).start()

    def cum_copy(r):
        return pltpu.make_async_remote_copy(
            src_ref=decay_in.at[0],
            dst_ref=cums.at[c],
            send_sem=cum_send.at[r],
            recv_sem=cum_recv.at[r],
            device_id={"ctx": flip(c, r)},
            device_id_type=MESH,
        )

    for r in range(1, CUBE):
        cum_copy(r).start()

    own_tok.wait()
    def own_start(ks):
        for k in ks:

            @pl.when(f < n_fsdp - 1)
            def _():
                w_copy(own_i, k, True).start()

            @pl.when(f > 0)
            def _():
                w_copy(own_i, k, False).start()

    tok_start(0, 0, 2)
    tok_start(0, 1, 4)

    @pl.when(owner)
    def _():
        for p in range(3):
            own_weight(p).wait()
        own_start(range(CHUNKS // 2))

    tok_start(0, 1, 2)
    tok_start(0, 0, 4)

    @pl.when(owner)
    def _():
        own_start(range(CHUNKS // 2, CHUNKS))

    tok_start(0, 0, 1)
    tok_start(0, 1, 1)

    inner = jnp.logical_and(f > 0, f < n_fsdp - 1)

    def inner_pass(i, ks):
        @pl.when(jnp.logical_and(inner, a * per_dev + i != f))
        def _():
            for k in ks:
                w_pass(i, k)

    def end_wait(i, ks):
        @pl.when(jnp.logical_and(f == 0, a * per_dev + i > f))
        def _():
            for k in ks:
                w_copy(i, k, True).wait_recv()

        @pl.when(jnp.logical_and(f == n_fsdp - 1, a * per_dev + i < f))
        def _():
            for k in ks:
                w_copy(i, k, False).wait_recv()

    far = 1 - first
    early, late = range(CHUNKS // 2), range(CHUNKS // 2, CHUNKS)
    def head_of(cc, i):
        return (cc % groups * per_dev + i) * shard_heads + cc // groups

    def columns(cc, i):
        return pl.ds(pl.multiple_of(head_of(cc, i) * hd, hd), hd)

    def out_copy(i, b):
        return pltpu.make_async_remote_copy(
            src_ref=stage.at[i, b],
            dst_ref=gat.at[:, columns(c, i)],
            send_sem=out_send.at[i, b],
            recv_sem=out_recv.at[i, c],
            device_id={"ctx": b},
            device_id_type=MESH,
        )

    t_pos = lax.broadcasted_iota(jnp.int32, (rows, rows), 0)
    u_pos = lax.broadcasted_iota(jnp.int32, (rows, rows), 1)
    def decays(n, _):
        i, b = n // CUBE, n % CUBE
        row = sums[i, pl.ds(b, 1), :]
        col = jnp.sum(jnp.where(t_pos == u_pos, row, 0.0), axis=1, keepdims=True)
        factors[i, b] = jnp.exp(jnp.where(t_pos >= u_pos, col - row, -jnp.inf))
        opening[i, b] = jnp.broadcast_to(jnp.exp(col), (rows, hd))
        closing[i, b] = jnp.broadcast_to(jnp.exp(row[:, rows - 1 :] - col), (rows, hd))
        return 0

    def activate(proj):
        qk = jax.nn.silu(proj[:, : 2 * hd]).astype(BF16)
        return jnp.concatenate([qk, proj[:, 2 * hd :].astype(BF16)], axis=1)

    def flipped(r):
        b = c
        bit = 1
        while bit < CUBE:
            b = b + ((r // bit) % 2) * (bit - 2 * bit * ((c // bit) % 2))
            bit *= 2
        return b

    def block_alone(i, b, qkv):
        q, k, v = qkv[:, :hd], qkv[:, hd : 2 * hd], qkv[:, 2 * hd :]
        scores = lax.dot_general(q, k, (((1,), (1,)), ((), ())), preferred_element_type=F32)
        weights = (scores * factors[i, b]).astype(BF16)
        inside = jnp.dot(weights, v, preferred_element_type=F32)
        scaled = (k.astype(F32) * closing[i, b]).astype(BF16)
        local = lax.dot_general(scaled, v, (((0,), (0,)), ((), ())), preferred_element_type=F32)
        return inside, local

    def chain(i, b, held, q, inside, local):
        incoming = jnp.dot(q, held.astype(BF16), preferred_element_type=F32) * opening[i, b]
        total = jnp.exp(sums[i, pl.ds(b, 1), :][:, rows - 1 :])
        state[...] = total * held + local
        stage[i, b] = (inside + incoming).astype(BF16)

    def send(i, b):
        @pl.when(b == c)
        def _():
            gat[:, columns(c, i)] = stage[i, b]

        @pl.when(b != c)
        def _():
            out_copy(i, b).start()

    def near_block(r, _):
        b = flipped(r)
        qkv = activate(jnp.dot(tok[b], w[first], preferred_element_type=F32))
        near_q[b] = qkv[:, :hd]
        near_inside[b], near_local[b] = block_alone(first, b, qkv)
        return 0

    def piece(b, lo, hi):
        at = pl.ds(lo * step, (hi - lo) * step)
        return jnp.dot(tok[b, :, at], w[far, at, :], preferred_element_type=F32)

    half_way, most = CHUNKS // 2, CHUNKS - CHUNKS // 4

    def grow(r, _):
        b = flipped(r)
        partial[b] = piece(b, 0, most)
        return 0

    def grow_first(b, _):
        partial[b] = piece(b, 0, half_way)
        return 0

    def grow_next(b, _):
        partial[b] += piece(b, half_way, most)
        return 0

    def finish(b):
        far_qkv[b % 2] = activate(partial[b] + piece(b, most, CHUNKS))

    inner_pass(first, early)
    tok_wait(2, 0)
    tok_start(2, 0, 4)
    tok_start(2, 0, 1)
    tok_wait(4, 1)
    tok_start(4, 1, 2)
    tok_start(4, 1, 1)
    for r in range(1, CUBE):
        pltpu.make_async_remote_copy(
            src_ref=decay_in.at[0],
            dst_ref=cums.at[flip(c, r)],
            send_sem=cum_send.at[r],
            recv_sem=cum_recv.at[r],
            device_id={"ctx": flip(c, r)},
            device_id_type=MESH,
        ).wait_recv()

    upto = jnp.where(t_pos <= u_pos, 1.0, 0.0).astype(F32)
    for i in range(per_dev):
        rates = jnp.concatenate(
            [cums[b, pl.ds(head_of(c, i), 1), :] for b in range(CUBE)], axis=0
        )
        sums[i] = jnp.dot(
            rates, upto, preferred_element_type=F32, precision=lax.Precision.HIGHEST
        )

    lax.fori_loop(0, per_dev * CUBE, decays, 0)
    inner_pass(first, late)
    inner_pass(far, early)
    tok_wait(2, 1)
    tok_start(2, 1, 1)
    tok_wait(4, 0)
    tok_start(4, 0, 1)
    inner_pass(far, late)
    end_wait(first, range(CHUNKS))
    for r in (1, 3, 5):
        for p in (0, 1):
            tok_wait(r, p)
    lax.fori_loop(0, 6, near_block, 0)

    @pl.when(inner)
    def _():
        lax.fori_loop(0, 6, grow, 0)

    tok_wait(6, 0)
    tok_start(6, 0, 1)
    tok_wait(6, 1)
    tok_start(6, 1, 1)
    for p in (0, 1):
        tok_wait(7, p)
    lax.fori_loop(6, CUBE, near_block, 0)

    state[...] = jnp.zeros_like(state)

    def near_one(b, _):
        chain(first, b, state[...], near_q[b], near_inside[b], near_local[b])
        send(first, b)
        return 0

    lax.fori_loop(0, CUBE, near_one, 0)

    @pl.when(inner)
    def _():
        lax.fori_loop(6, CUBE, grow, 0)

    @pl.when(jnp.logical_not(inner))
    def _():
        end_wait(far, range(half_way))
        lax.fori_loop(0, CUBE, grow_first, 0)
        end_wait(far, range(half_way, most))
        lax.fori_loop(0, CUBE, grow_next, 0)
        end_wait(far, range(most, CHUNKS))

    finish(0)
    state[...] = jnp.zeros_like(state)

    def far_block(b, ahead):
        qkv, held = far_qkv[b % 2], state[...]
        if ahead:
            finish(b + 1)
        inside, local = block_alone(far, b, qkv)
        chain(far, b, held, qkv[:, :hd], inside, local)
        send(far, b)

    def far_one(b, _):
        far_block(b, True)
        return 0

    lax.fori_loop(0, CUBE - 1, far_one, 0)
    far_block(CUBE - 1, False)

    for copy in sent:
        copy.wait_send()
    for r in range(1, CUBE):
        cum_copy(r).wait_send()
    for i in range(per_dev):
        for k in range(CHUNKS):

            @pl.when(goes_up(i))
            def _():
                w_copy(i, k, True).wait_send()

            @pl.when(goes_down(i))
            def _():
                w_copy(i, k, False).wait_send()

    for i in range(per_dev):
        for r in range(1, CUBE):
            peer = flip(c, r)
            pltpu.make_async_remote_copy(
                src_ref=stage.at[i, peer],
                dst_ref=gat.at[:, columns(peer, i)],
                send_sem=out_send.at[i, peer],
                recv_sem=out_recv.at[i, peer],
                device_id={"ctx": peer},
                device_id_type=MESH,
            ).wait()

    band = 32

    def norm(n, _):
        at = pl.ds(pl.multiple_of(n * band, band), band)
        x = gat[at, :].astype(F32)
        mean_sq = jnp.sum(x * x, axis=1, keepdims=True) / feats
        out_ref[0, at, :] = (x * lax.rsqrt(mean_sq + 1e-05) * gain_ref[...]).astype(BF16)
        return 0

    lax.fori_loop(0, rows // band, norm, 0)


def head_body(n_ctx, n_fsdp, tokens, qkv_weight, log_decay, norm_gain):
    rows, depth = tokens.shape[1:]
    heads = log_decay.shape[1]
    feats = norm_gain.shape[0]
    hd = feats // heads
    per_dev = heads // n_ctx
    dims = (n_fsdp, heads // n_fsdp, per_dev, hd, feats)
    dma = pltpu.SemaphoreType.DMA
    vmem = pl.BlockSpec(memory_space=pltpu.VMEM)
    hbm = pl.BlockSpec(memory_space=pl.ANY)
    normed = pl.pallas_call(
        functools.partial(head_kernel, dims),
        out_shape=jax.ShapeDtypeStruct((1, rows, feats), BF16),
        in_specs=[hbm, hbm, vmem, vmem],
        out_specs=vmem,
        scratch_shapes=[
            pltpu.VMEM((n_ctx, rows, depth), BF16),
            pltpu.VMEM((per_dev, depth, 3 * hd), BF16),
            pltpu.VMEM((n_ctx, heads, rows), F32),
            pltpu.VMEM((per_dev, n_ctx, rows, hd), BF16),
            pltpu.VMEM((rows, feats), BF16),
            pltpu.VMEM((hd, hd), F32),
            pltpu.VMEM((per_dev, n_ctx, rows), F32),
            pltpu.VMEM((per_dev, n_ctx, rows, rows), F32),
            pltpu.VMEM((per_dev, n_ctx, rows, hd), F32),
            pltpu.VMEM((per_dev, n_ctx, rows, hd), F32),
            pltpu.VMEM((n_ctx, rows, hd), BF16),
            pltpu.VMEM((n_ctx, rows, hd), F32),
            pltpu.VMEM((n_ctx, hd, hd), F32),
            pltpu.VMEM((2, rows, 3 * hd), BF16),
            pltpu.VMEM((n_ctx, rows, 3 * hd), F32),
            dma((4,)),
            dma((CUBE, 2, 3)),
            dma((CUBE, 2)),
            dma((per_dev, CHUNKS)),
            dma((per_dev, CHUNKS)),
            dma((per_dev, CHUNKS)),
            dma((CUBE,)),
            dma((CUBE,)),
            dma((per_dev, n_ctx)),
            dma((per_dev, n_ctx)),
        ],
        compiler_params=pltpu.CompilerParams(
            collective_id=0, has_side_effects=True, vmem_limit_bytes=56 * 1024 * 1024
        ),
        cost_estimate=pl.CostEstimate(
            flops=6 * rows * depth * feats, bytes_accessed=16 * rows * feats, transcendentals=0
        ),
    )(tokens, qkv_weight, log_decay, norm_gain[None])
    return normed


def entering(part, axis, combine, identity):
    place = lax.axis_index(axis)
    gathered = jax.tree.map(lambda a: lax.all_gather(a, axis), part)
    state = jax.tree.map(lambda a, e: jnp.zeros_like(a) + jnp.asarray(e, a.dtype), part, identity)

    def one(turn, state):
        return combine(
            state, jax.tree.map(lambda a: lax.dynamic_index_in_dim(a, turn, 0, False), gathered)
        )

    return lax.fori_loop(0, place, one, state)


def chain_states(decay_total, local):

    def combine(earlier, later):
        return (earlier[0] * later[0], later[0][:, None, None] * earlier[1] + later[1])

    identity_pair = (jnp.ones_like(decay_total), jnp.zeros_like(local))
    return entering((decay_total, local), "ctx", combine, identity_pair)[1]


def segment_memory_matrix(keys, values, cumulative):
    tail = jnp.exp(cumulative[:, -1:] - cumulative)
    weighted_key_vectors = (keys.astype(jnp.float32) * tail.T[:, :, None]).astype(jnp.bfloat16)
    local = jnp.einsum(
        "thd,the->hde", weighted_key_vectors, values, preferred_element_type=jnp.float32
    )
    return (jnp.exp(cumulative[:, -1]), local)


def body(tokens, qkv_weight, log_decay, norm_gain):
    inputs = tokens[0]
    log_rates = log_decay[0]
    head_count = log_rates.shape[0]
    span_len = log_rates.shape[1]
    feat_total = norm_gain.shape[0]
    head_dimension = feat_total // head_count

    def project(piece):
        return jnp.einsum("td,cde->cte", inputs, piece, preferred_element_type=jnp.float32)

    cumulative = jnp.cumsum(log_rates, axis=1)
    paired = project(lax.all_gather(qkv_weight[1:], "fsdp", axis=2, tiled=True))
    keys = jax.nn.silu(paired[0]).astype(jnp.bfloat16).reshape(span_len, head_count, head_dimension)
    values = paired[1].astype(jnp.bfloat16).reshape(span_len, head_count, head_dimension)
    decay_total, local = segment_memory_matrix(keys, values, cumulative)
    carried = chain_states(decay_total, local)
    asked = project(lax.all_gather(qkv_weight[:1], "fsdp", axis=2, tiled=True))
    queries = (
        jax.nn.silu(asked[0]).astype(jnp.bfloat16).reshape(span_len, head_count, head_dimension)
    )
    log_gaps = cumulative[:, :, None] - cumulative[:, None, :]
    causal = jnp.arange(span_len)[:, None] >= jnp.arange(span_len)[None, :]
    factors = jnp.exp(jnp.where(causal[None], log_gaps, -jnp.inf))
    scores = jnp.einsum("thd,shd->hts", queries, keys, preferred_element_type=jnp.float32)
    weights = (scores * factors).astype(jnp.bfloat16)
    inside = jnp.einsum("hts,shd->thd", weights, values, preferred_element_type=jnp.float32)
    reduced_precision_memory = carried.astype(jnp.bfloat16)
    incoming = jnp.einsum(
        "thd,hde->the", queries, reduced_precision_memory, preferred_element_type=jnp.float32
    )
    incoming = incoming * jnp.exp(cumulative).T[:, :, None]
    attention_output = (inside + incoming).reshape(span_len, feat_total)
    mean_sq = jnp.mean(attention_output * attention_output, axis=-1, keepdims=True)
    normed = (attention_output * lax.rsqrt(mean_sq + 1e-05) * norm_gain).astype(jnp.bfloat16)
    return normed[None]


def solution(mesh):
    placed = (P("fsdp", "ctx", None), P(None, None, "fsdp"), P("fsdp", None, "ctx"), P())
    n_ctx, n_fsdp = mesh.shape["ctx"], mesh.shape["fsdp"]

    def run(tokens, qkv_weight, log_decay, norm_gain):
        heads = log_decay.shape[1]
        by_head = n_ctx == CUBE and heads == 2 * n_ctx and n_fsdp % 2 == 0 and heads % n_fsdp == 0
        chosen = functools.partial(head_body, n_ctx, n_fsdp) if by_head else body
        return chosen(tokens, qkv_weight, log_decay, norm_gain)

    return jax.shard_map(
        run, mesh=mesh, in_specs=placed, out_specs=P("fsdp", "ctx", None), check_vma=False
    )
```

```python
import functools
import jax
import jax.numpy as jnp
from jax import lax
from jax.experimental import pallas as pl
from jax.experimental.pallas import tpu as pltpu
from jax.sharding import PartitionSpec as P

MESH = pl.DeviceIdType.MESH
CUBE = 8
CHUNKS = 8
F32 = jnp.float32
BF16 = jnp.bfloat16


def flip(c, r):
    out = c
    bit = 1
    while bit < CUBE:
        if r & bit:
            out = out + bit - 2 * bit * ((c // bit) % 2)
        bit *= 2
    return out


def head_kernel(
    dims,
    tok_in,
    w_in,
    decay_in,
    gain_ref,
    out_ref,
    tok,
    w,
    cums,
    stage,
    gat,
    state,
    sums,
    factors,
    opening,
    closing,
    near_q,
    near_inside,
    near_local,
    far_qkv,
    partial,
    local_sem,
    tok_send,
    tok_recv,
    w_up,
    w_down,
    w_recv,
    cum_send,
    cum_recv,
    out_send,
    out_recv,
):
    n_fsdp, shard_heads, per_dev, hd, feats = dims
    groups = n_fsdp // per_dev
    c = lax.axis_index("ctx")
    f = lax.axis_index("fsdp")
    j, a = c // groups, c % groups
    rows = tok.shape[1]
    half = rows // 2
    depth = w.shape[1]
    step = depth // CHUNKS

    first = jnp.where(f > a * per_dev, 1, 0)

    own_tok = pltpu.make_async_copy(tok_in.at[0], tok.at[c], local_sem.at[0])
    own_tok.start()
    cums[c] = decay_in[0]
    owner = f // per_dev == a
    own_i = f % per_dev

    def own_weight(p):
        return pltpu.make_async_copy(
            w_in.at[p, :, pl.ds(pl.multiple_of(j * hd, hd), hd)],
            w.at[own_i, :, pl.ds(p * hd, hd)],
            local_sem.at[1 + p],
        )

    @pl.when(owner)
    def _():
        for p in range(3):
            own_weight(p).start()

    barrier = pltpu.get_barrier_semaphore()
    for r in range(1, CUBE):
        pl.semaphore_signal(barrier, inc=1, device_id={"ctx": flip(c, r)}, device_id_type=MESH)

    @pl.when(f > 0)
    def _():
        pl.semaphore_signal(barrier, inc=1, device_id={"fsdp": f - 1}, device_id_type=MESH)

    @pl.when(f < n_fsdp - 1)
    def _():
        pl.semaphore_signal(barrier, inc=1, device_id={"fsdp": f + 1}, device_id_type=MESH)

    ends = jnp.where(f > 0, 1, 0) + jnp.where(f < n_fsdp - 1, 1, 0)
    pl.semaphore_wait(barrier, CUBE - 1 + ends)

    def tok_copy(r, p, d):
        part = tok.at[flip(c, r), pl.ds(p * half, half), :]
        return pltpu.make_async_remote_copy(
            src_ref=part,
            dst_ref=part,
            send_sem=tok_send.at[r, p, (1, 2, 4).index(d)],
            recv_sem=tok_recv.at[r ^ d, p],
            device_id={"ctx": flip(c, d)},
            device_id_type=MESH,
        )

    def tok_wait(r, p):
        part = tok.at[flip(c, r), pl.ds(p * half, half), :]
        pltpu.make_async_remote_copy(
            src_ref=part,
            dst_ref=part,
            send_sem=tok_send.at[r, p, 0],
            recv_sem=tok_recv.at[r, p],
            device_id={"ctx": flip(c, 1)},
            device_id_type=MESH,
        ).wait_recv()

    sent = []

    def tok_start(r, p, d):
        copy = tok_copy(r, p, d)
        copy.start()
        sent.append(copy)

    def w_copy(i, k, up):
        part = w.at[i, pl.ds(pl.multiple_of(k * step, step), step), :]
        return pltpu.make_async_remote_copy(
            src_ref=part,
            dst_ref=part,
            send_sem=(w_up if up else w_down).at[i, k],
            recv_sem=w_recv.at[i, k],
            device_id={"fsdp": f + 1 if up else f - 1},
            device_id_type=MESH,
        )

    def goes_up(i):
        return jnp.logical_and(a * per_dev + i <= f, f < n_fsdp - 1)

    def goes_down(i):
        return jnp.logical_and(a * per_dev + i >= f, f > 0)

    def w_pass(i, k):
        @pl.when(a * per_dev + i < f)
        def _():
            w_copy(i, k, False).wait_recv()

        @pl.when(a * per_dev + i > f)
        def _():
            w_copy(i, k, True).wait_recv()

        @pl.when(goes_up(i))
        def _():
            w_copy(i, k, True).start()

        @pl.when(goes_down(i))
        def _():
            w_copy(i, k, False).start()

    def cum_copy(r):
        return pltpu.make_async_remote_copy(
            src_ref=decay_in.at[0],
            dst_ref=cums.at[c],
            send_sem=cum_send.at[r],
            recv_sem=cum_recv.at[r],
            device_id={"ctx": flip(c, r)},
            device_id_type=MESH,
        )

    for r in range(1, CUBE):
        cum_copy(r).start()

    own_tok.wait()
    def own_start(ks):
        for k in ks:

            @pl.when(f < n_fsdp - 1)
            def _():
                w_copy(own_i, k, True).start()

            @pl.when(f > 0)
            def _():
                w_copy(own_i, k, False).start()

    @pl.when(owner)
    def _():
        for p in range(3):
            own_weight(p).wait()
        own_start(range(CHUNKS))

    for p, d in ((0, 2), (1, 4), (1, 2), (0, 4), (0, 1), (1, 1)):
        tok_start(0, p, d)

    inner = jnp.logical_and(f > 0, f < n_fsdp - 1)

    def inner_pass(i, ks):
        @pl.when(jnp.logical_and(inner, a * per_dev + i != f))
        def _():
            for k in ks:
                w_pass(i, k)

    def end_wait(i, ks):
        @pl.when(jnp.logical_and(f == 0, a * per_dev + i > f))
        def _():
            for k in ks:
                w_copy(i, k, True).wait_recv()

        @pl.when(jnp.logical_and(f == n_fsdp - 1, a * per_dev + i < f))
        def _():
            for k in ks:
                w_copy(i, k, False).wait_recv()

    far = 1 - first
    early, late = range(CHUNKS // 2), range(CHUNKS // 2, CHUNKS)
    def head_of(cc, i):
        return (cc % groups * per_dev + i) * shard_heads + cc // groups

    def columns(cc, i):
        return pl.ds(pl.multiple_of(head_of(cc, i) * hd, hd), hd)

    def out_copy(i, b):
        return pltpu.make_async_remote_copy(
            src_ref=stage.at[i, b],
            dst_ref=gat.at[:, columns(c, i)],
            send_sem=out_send.at[i, b],
            recv_sem=out_recv.at[i, c],
            device_id={"ctx": b},
            device_id_type=MESH,
        )

    t_pos = lax.broadcasted_iota(jnp.int32, (rows, rows), 0)
    u_pos = lax.broadcasted_iota(jnp.int32, (rows, rows), 1)
    def add_up():
        for r in range(1, CUBE):
            pltpu.make_async_remote_copy(
                src_ref=decay_in.at[0],
                dst_ref=cums.at[flip(c, r)],
                send_sem=cum_send.at[r],
                recv_sem=cum_recv.at[r],
                device_id={"ctx": flip(c, r)},
                device_id_type=MESH,
            ).wait_recv()

        upto = jnp.where(t_pos <= u_pos, 1.0, 0.0).astype(F32)
        for i in range(per_dev):
            rates = jnp.concatenate(
                [cums[b, pl.ds(head_of(c, i), 1), :] for b in range(CUBE)], axis=0
            )
            sums[i] = jnp.dot(
                rates, upto, preferred_element_type=F32, precision=lax.Precision.HIGHEST
            )

    def decays_of(i, b):
        row = sums[i, pl.ds(b, 1), :]
        col = jnp.sum(jnp.where(t_pos == u_pos, row, 0.0), axis=1, keepdims=True)
        inside = jnp.exp(jnp.where(t_pos >= u_pos, col - row, -jnp.inf))
        return inside, jnp.exp(col), jnp.exp(row[:, rows - 1 :] - col)

    def decays(n, _):
        i, b = n // CUBE, n % CUBE
        inside, opens, closes = decays_of(i, b)
        factors[i, b] = inside
        opening[i, b] = jnp.broadcast_to(opens, (rows, hd))
        closing[i, b] = jnp.broadcast_to(closes, (rows, hd))
        return 0

    def activate(proj):
        qk = jax.nn.silu(proj[:, : 2 * hd]).astype(BF16)
        return jnp.concatenate([qk, proj[:, 2 * hd :].astype(BF16)], axis=1)

    def flipped(r):
        b = c
        bit = 1
        while bit < CUBE:
            b = b + ((r // bit) % 2) * (bit - 2 * bit * ((c // bit) % 2))
            bit *= 2
        return b

    def block_alone(qkv, factor, close):
        q, k, v = qkv[:, :hd], qkv[:, hd : 2 * hd], qkv[:, 2 * hd :]
        scores = lax.dot_general(q, k, (((1,), (1,)), ((), ())), preferred_element_type=F32)
        weights = (scores * factor).astype(BF16)
        inside = jnp.dot(weights, v, preferred_element_type=F32)
        scaled = (k.astype(F32) * close).astype(BF16)
        local = lax.dot_general(scaled, v, (((0,), (0,)), ((), ())), preferred_element_type=F32)
        return inside, local

    def chain(i, b, held, q, inside, local, opens):
        incoming = jnp.dot(q, held.astype(BF16), preferred_element_type=F32) * opens
        total = jnp.exp(sums[i, pl.ds(b, 1), :][:, rows - 1 :])
        state[...] = total * held + local
        stage[i, b] = (inside + incoming).astype(BF16)

    def send(i, b):
        @pl.when(b == c)
        def _():
            gat[:, columns(c, i)] = stage[i, b]

        @pl.when(b != c)
        def _():
            out_copy(i, b).start()

    def near_block(r, _):
        b = flipped(r)
        qkv = activate(jnp.dot(tok[b], w[first], preferred_element_type=F32))
        near_q[b] = qkv[:, :hd]
        near_inside[b], near_local[b] = block_alone(qkv, factors[first, b], closing[first, b])
        return 0

    def piece(b, lo, hi):
        at = pl.ds(lo * step, (hi - lo) * step)
        return jnp.dot(tok[b, :, at], w[far, at, :], preferred_element_type=F32)

    half_way, most = CHUNKS // 2, CHUNKS - CHUNKS // 4

    def grow_first(b, _):
        partial[b] = piece(b, 0, half_way)
        return 0

    def grow_next(b, _):
        partial[b] += piece(b, half_way, most)
        return 0

    def finish(b):
        far_qkv[b % 2] = activate(partial[b] + piece(b, most, CHUNKS))

    def end_plane():
        lax.fori_loop(6, CUBE, near_block, 0)

        state[...] = jnp.zeros_like(state)

        def near_one(b, _):
            given = near_q[b], near_inside[b], near_local[b], opening[first, b]
            chain(first, b, state[...], *given)
            send(first, b)
            return 0

        lax.fori_loop(0, CUBE, near_one, 0)

        end_wait(far, range(half_way))
        lax.fori_loop(0, CUBE, grow_first, 0)
        end_wait(far, range(half_way, most))
        lax.fori_loop(0, CUBE, grow_next, 0)
        end_wait(far, range(most, CHUNKS))

        finish(0)
        state[...] = jnp.zeros_like(state)

        def far_block(b, ahead):
            qkv, held = far_qkv[b % 2], state[...]
            if ahead:
                finish(b + 1)
            inside, local = block_alone(qkv, factors[far, b], closing[far, b])
            chain(far, b, held, qkv[:, :hd], inside, local, opening[far, b])
            send(far, b)

        def far_one(b, _):
            far_block(b, True)
            return 0

        lax.fori_loop(0, CUBE - 1, far_one, 0)
        far_block(CUBE - 1, False)

    def place(t):
        return first + (1 - 2 * first) * (t // CUBE), t % CUBE

    def project(t):
        i, b = place(t)
        return jnp.dot(tok[b], w[i], preferred_element_type=F32)

    def inner_block(t, ahead):
        i, b = place(t)

        @pl.when(b == 0)
        def _():
            state[...] = jnp.zeros_like(state)

        qkv, held = far_qkv[t % 2], state[...]
        proj = project(t + 1) if ahead else None
        factor, opens, closes = decays_of(i, b)
        inside, local = block_alone(qkv, factor, closes)
        chain(i, b, held, qkv[:, :hd], inside, local, opens)
        if ahead:
            far_qkv[(t + 1) % 2] = activate(proj)
        send(i, b)

    def inner_one(t, _):
        inner_block(t, True)
        return 0

    def inner_plane():
        far_qkv[0] = activate(project(0))
        lax.fori_loop(0, per_dev * CUBE - 1, inner_one, 0)
        inner_block(per_dev * CUBE - 1, False)

    inner_pass(first, early)
    tok_wait(2, 0)
    tok_start(2, 0, 4)
    tok_start(2, 0, 1)
    tok_wait(4, 1)
    tok_start(4, 1, 2)
    tok_start(4, 1, 1)
    @pl.when(jnp.logical_not(inner))
    def _():
        add_up()
        lax.fori_loop(0, per_dev * CUBE, decays, 0)

    inner_pass(first, late)
    inner_pass(far, early)
    tok_wait(2, 1)
    tok_start(2, 1, 1)
    tok_wait(4, 0)
    tok_start(4, 0, 1)
    inner_pass(far, late)
    end_wait(first, range(CHUNKS))
    for r in (1, 3, 5):
        for p in (0, 1):
            tok_wait(r, p)
    @pl.when(inner)
    def _():
        add_up()

    @pl.when(jnp.logical_not(inner))
    def _():
        lax.fori_loop(0, 6, near_block, 0)

    tok_wait(6, 0)
    tok_start(6, 0, 1)
    tok_wait(6, 1)
    tok_start(6, 1, 1)
    for p in (0, 1):
        tok_wait(7, p)
    @pl.when(jnp.logical_not(inner))
    def _():
        end_plane()

    @pl.when(inner)
    def _():
        inner_plane()

    for copy in sent:
        copy.wait_send()
    for r in range(1, CUBE):
        cum_copy(r).wait_send()
    for i in range(per_dev):
        for k in range(CHUNKS):

            @pl.when(goes_up(i))
            def _():
                w_copy(i, k, True).wait_send()

            @pl.when(goes_down(i))
            def _():
                w_copy(i, k, False).wait_send()

    for i in range(per_dev):
        for r in range(1, CUBE):
            peer = flip(c, r)
            pltpu.make_async_remote_copy(
                src_ref=stage.at[i, peer],
                dst_ref=gat.at[:, columns(peer, i)],
                send_sem=out_send.at[i, peer],
                recv_sem=out_recv.at[i, peer],
                device_id={"ctx": peer},
                device_id_type=MESH,
            ).wait()

    band = 32

    def norm(n, _):
        at = pl.ds(pl.multiple_of(n * band, band), band)
        x = gat[at, :].astype(F32)
        mean_sq = jnp.sum(x * x, axis=1, keepdims=True) / feats
        out_ref[0, at, :] = (x * lax.rsqrt(mean_sq + 1e-05) * gain_ref[...]).astype(BF16)
        return 0

    lax.fori_loop(0, rows // band, norm, 0)


def head_body(n_ctx, n_fsdp, tokens, qkv_weight, log_decay, norm_gain):
    rows, depth = tokens.shape[1:]
    heads = log_decay.shape[1]
    feats = norm_gain.shape[0]
    hd = feats // heads
    per_dev = heads // n_ctx
    dims = (n_fsdp, heads // n_fsdp, per_dev, hd, feats)
    dma = pltpu.SemaphoreType.DMA
    vmem = pl.BlockSpec(memory_space=pltpu.VMEM)
    hbm = pl.BlockSpec(memory_space=pl.ANY)
    normed = pl.pallas_call(
        functools.partial(head_kernel, dims),
        out_shape=jax.ShapeDtypeStruct((1, rows, feats), BF16),
        in_specs=[hbm, hbm, vmem, vmem],
        out_specs=vmem,
        scratch_shapes=[
            pltpu.VMEM((n_ctx, rows, depth), BF16),
            pltpu.VMEM((per_dev, depth, 3 * hd), BF16),
            pltpu.VMEM((n_ctx, heads, rows), F32),
            pltpu.VMEM((per_dev, n_ctx, rows, hd), BF16),
            pltpu.VMEM((rows, feats), BF16),
            pltpu.VMEM((hd, hd), F32),
            pltpu.VMEM((per_dev, n_ctx, rows), F32),
            pltpu.VMEM((per_dev, n_ctx, rows, rows), F32),
            pltpu.VMEM((per_dev, n_ctx, rows, hd), F32),
            pltpu.VMEM((per_dev, n_ctx, rows, hd), F32),
            pltpu.VMEM((n_ctx, rows, hd), BF16),
            pltpu.VMEM((n_ctx, rows, hd), F32),
            pltpu.VMEM((n_ctx, hd, hd), F32),
            pltpu.VMEM((2, rows, 3 * hd), BF16),
            pltpu.VMEM((n_ctx, rows, 3 * hd), F32),
            dma((4,)),
            dma((CUBE, 2, 3)),
            dma((CUBE, 2)),
            dma((per_dev, CHUNKS)),
            dma((per_dev, CHUNKS)),
            dma((per_dev, CHUNKS)),
            dma((CUBE,)),
            dma((CUBE,)),
            dma((per_dev, n_ctx)),
            dma((per_dev, n_ctx)),
        ],
        compiler_params=pltpu.CompilerParams(
            collective_id=0, has_side_effects=True, vmem_limit_bytes=56 * 1024 * 1024
        ),
        cost_estimate=pl.CostEstimate(
            flops=6 * rows * depth * feats, bytes_accessed=16 * rows * feats, transcendentals=0
        ),
    )(tokens, qkv_weight, log_decay, norm_gain[None])
    return normed


def entering(part, axis, combine, identity):
    place = lax.axis_index(axis)
    gathered = jax.tree.map(lambda a: lax.all_gather(a, axis), part)
    state = jax.tree.map(lambda a, e: jnp.zeros_like(a) + jnp.asarray(e, a.dtype), part, identity)

    def one(turn, state):
        return combine(
            state, jax.tree.map(lambda a: lax.dynamic_index_in_dim(a, turn, 0, False), gathered)
        )

    return lax.fori_loop(0, place, one, state)


def chain_states(decay_total, local):

    def combine(earlier, later):
        return (earlier[0] * later[0], later[0][:, None, None] * earlier[1] + later[1])

    identity_pair = (jnp.ones_like(decay_total), jnp.zeros_like(local))
    return entering((decay_total, local), "ctx", combine, identity_pair)[1]


def segment_memory_matrix(keys, values, cumulative):
    tail = jnp.exp(cumulative[:, -1:] - cumulative)
    weighted_key_vectors = (keys.astype(jnp.float32) * tail.T[:, :, None]).astype(jnp.bfloat16)
    local = jnp.einsum(
        "thd,the->hde", weighted_key_vectors, values, preferred_element_type=jnp.float32
    )
    return (jnp.exp(cumulative[:, -1]), local)


def body(tokens, qkv_weight, log_decay, norm_gain):
    inputs = tokens[0]
    log_rates = log_decay[0]
    head_count = log_rates.shape[0]
    span_len = log_rates.shape[1]
    feat_total = norm_gain.shape[0]
    head_dimension = feat_total // head_count

    def project(piece):
        return jnp.einsum("td,cde->cte", inputs, piece, preferred_element_type=jnp.float32)

    cumulative = jnp.cumsum(log_rates, axis=1)
    paired = project(lax.all_gather(qkv_weight[1:], "fsdp", axis=2, tiled=True))
    keys = jax.nn.silu(paired[0]).astype(jnp.bfloat16).reshape(span_len, head_count, head_dimension)
    values = paired[1].astype(jnp.bfloat16).reshape(span_len, head_count, head_dimension)
    decay_total, local = segment_memory_matrix(keys, values, cumulative)
    carried = chain_states(decay_total, local)
    asked = project(lax.all_gather(qkv_weight[:1], "fsdp", axis=2, tiled=True))
    queries = (
        jax.nn.silu(asked[0]).astype(jnp.bfloat16).reshape(span_len, head_count, head_dimension)
    )
    log_gaps = cumulative[:, :, None] - cumulative[:, None, :]
    causal = jnp.arange(span_len)[:, None] >= jnp.arange(span_len)[None, :]
    factors = jnp.exp(jnp.where(causal[None], log_gaps, -jnp.inf))
    scores = jnp.einsum("thd,shd->hts", queries, keys, preferred_element_type=jnp.float32)
    weights = (scores * factors).astype(jnp.bfloat16)
    inside = jnp.einsum("hts,shd->thd", weights, values, preferred_element_type=jnp.float32)
    reduced_precision_memory = carried.astype(jnp.bfloat16)
    incoming = jnp.einsum(
        "thd,hde->the", queries, reduced_precision_memory, preferred_element_type=jnp.float32
    )
    incoming = incoming * jnp.exp(cumulative).T[:, :, None]
    attention_output = (inside + incoming).reshape(span_len, feat_total)
    mean_sq = jnp.mean(attention_output * attention_output, axis=-1, keepdims=True)
    normed = (attention_output * lax.rsqrt(mean_sq + 1e-05) * norm_gain).astype(jnp.bfloat16)
    return normed[None]


def solution(mesh):
    placed = (P("fsdp", "ctx", None), P(None, None, "fsdp"), P("fsdp", None, "ctx"), P())
    n_ctx, n_fsdp = mesh.shape["ctx"], mesh.shape["fsdp"]

    def run(tokens, qkv_weight, log_decay, norm_gain):
        heads = log_decay.shape[1]
        by_head = n_ctx == CUBE and heads == 2 * n_ctx and n_fsdp % 2 == 0 and heads % n_fsdp == 0
        chosen = functools.partial(head_body, n_ctx, n_fsdp) if by_head else body
        return chosen(tokens, qkv_weight, log_decay, norm_gain)

    return jax.shard_map(
        run, mesh=mesh, in_specs=placed, out_specs=P("fsdp", "ctx", None), check_vma=False
    )
```

```python
import functools
import jax
import jax.numpy as jnp
from jax import lax
from jax.experimental import pallas as pl
from jax.experimental.pallas import tpu as pltpu
from jax.sharding import PartitionSpec as P

MESH = pl.DeviceIdType.MESH
CUBE = 8
CHUNKS = 8
F32 = jnp.float32
BF16 = jnp.bfloat16


def flip(c, r):
    out = c
    bit = 1
    while bit < CUBE:
        if r & bit:
            out = out + bit - 2 * bit * ((c // bit) % 2)
        bit *= 2
    return out


def head_kernel(
    dims,
    tok_in,
    w_in,
    decay_in,
    gain_ref,
    out_ref,
    tok,
    w,
    cums,
    stage,
    gat,
    state,
    sums,
    factors,
    opening,
    closing,
    near_q,
    near_inside,
    near_local,
    far_qkv,
    partial,
    local_sem,
    tok_send,
    tok_recv,
    w_up,
    w_down,
    w_recv,
    cum_send,
    cum_recv,
    out_send,
    out_recv,
):
    n_fsdp, shard_heads, per_dev, hd, feats = dims
    groups = n_fsdp // per_dev
    c = lax.axis_index("ctx")
    f = lax.axis_index("fsdp")
    j, a = c // groups, c % groups
    rows = tok.shape[1]
    half = rows // 2
    depth = w.shape[1]
    step = depth // CHUNKS

    first = jnp.where(f > a * per_dev, 1, 0)

    own_tok = pltpu.make_async_copy(tok_in.at[0], tok.at[c], local_sem.at[0])
    own_tok.start()
    cums[c] = decay_in[0]
    owner = f // per_dev == a
    own_i = f % per_dev

    def own_weight(p):
        return pltpu.make_async_copy(
            w_in.at[p, :, pl.ds(pl.multiple_of(j * hd, hd), hd)],
            w.at[own_i, :, pl.ds(p * hd, hd)],
            local_sem.at[1 + p],
        )

    @pl.when(owner)
    def _():
        for p in range(3):
            own_weight(p).start()

    barrier = pltpu.get_barrier_semaphore()
    for r in range(1, CUBE):
        pl.semaphore_signal(barrier, inc=1, device_id={"ctx": flip(c, r)}, device_id_type=MESH)

    @pl.when(f > 0)
    def _():
        pl.semaphore_signal(barrier, inc=1, device_id={"fsdp": f - 1}, device_id_type=MESH)

    @pl.when(f < n_fsdp - 1)
    def _():
        pl.semaphore_signal(barrier, inc=1, device_id={"fsdp": f + 1}, device_id_type=MESH)

    ends = jnp.where(f > 0, 1, 0) + jnp.where(f < n_fsdp - 1, 1, 0)
    pl.semaphore_wait(barrier, CUBE - 1 + ends)

    def tok_copy(r, p, d):
        part = tok.at[flip(c, r), pl.ds(p * half, half), :]
        return pltpu.make_async_remote_copy(
            src_ref=part,
            dst_ref=part,
            send_sem=tok_send.at[r, p, (1, 2, 4).index(d)],
            recv_sem=tok_recv.at[r ^ d, p],
            device_id={"ctx": flip(c, d)},
            device_id_type=MESH,
        )

    def tok_wait(r, p):
        part = tok.at[flip(c, r), pl.ds(p * half, half), :]
        pltpu.make_async_remote_copy(
            src_ref=part,
            dst_ref=part,
            send_sem=tok_send.at[r, p, 0],
            recv_sem=tok_recv.at[r, p],
            device_id={"ctx": flip(c, 1)},
            device_id_type=MESH,
        ).wait_recv()

    sent = []

    def tok_start(r, p, d):
        copy = tok_copy(r, p, d)
        copy.start()
        sent.append(copy)

    def w_copy(i, k, up):
        part = w.at[i, pl.ds(pl.multiple_of(k * step, step), step), :]
        return pltpu.make_async_remote_copy(
            src_ref=part,
            dst_ref=part,
            send_sem=(w_up if up else w_down).at[i, k],
            recv_sem=w_recv.at[i, k],
            device_id={"fsdp": f + 1 if up else f - 1},
            device_id_type=MESH,
        )

    def goes_up(i):
        return jnp.logical_and(a * per_dev + i <= f, f < n_fsdp - 1)

    def goes_down(i):
        return jnp.logical_and(a * per_dev + i >= f, f > 0)

    def w_pass(i, k):
        @pl.when(a * per_dev + i < f)
        def _():
            w_copy(i, k, False).wait_recv()

        @pl.when(a * per_dev + i > f)
        def _():
            w_copy(i, k, True).wait_recv()

        @pl.when(goes_up(i))
        def _():
            w_copy(i, k, True).start()

        @pl.when(goes_down(i))
        def _():
            w_copy(i, k, False).start()

    def cum_copy(r):
        return pltpu.make_async_remote_copy(
            src_ref=decay_in.at[0],
            dst_ref=cums.at[c],
            send_sem=cum_send.at[r],
            recv_sem=cum_recv.at[r],
            device_id={"ctx": flip(c, r)},
            device_id_type=MESH,
        )

    for r in range(1, CUBE):
        cum_copy(r).start()

    own_tok.wait()
    def own_start(ks):
        for k in ks:

            @pl.when(f < n_fsdp - 1)
            def _():
                w_copy(own_i, k, True).start()

            @pl.when(f > 0)
            def _():
                w_copy(own_i, k, False).start()

    @pl.when(owner)
    def _():
        for p in range(3):
            own_weight(p).wait()
        own_start(range(CHUNKS))

    for p, d in ((0, 2), (1, 4), (1, 2), (0, 4), (0, 1), (1, 1)):
        tok_start(0, p, d)

    inner = jnp.logical_and(f > 0, f < n_fsdp - 1)

    def inner_pass(i, ks):
        @pl.when(jnp.logical_and(inner, a * per_dev + i != f))
        def _():
            for k in ks:
                w_pass(i, k)

    def end_wait(i, ks):
        @pl.when(jnp.logical_and(f == 0, a * per_dev + i > f))
        def _():
            for k in ks:
                w_copy(i, k, True).wait_recv()

        @pl.when(jnp.logical_and(f == n_fsdp - 1, a * per_dev + i < f))
        def _():
            for k in ks:
                w_copy(i, k, False).wait_recv()

    far = 1 - first
    early, late = range(CHUNKS // 2), range(CHUNKS // 2, CHUNKS)
    def head_of(cc, i):
        return (cc % groups * per_dev + i) * shard_heads + cc // groups

    def columns(cc, i):
        return pl.ds(pl.multiple_of(head_of(cc, i) * hd, hd), hd)

    def out_copy(i, b):
        return pltpu.make_async_remote_copy(
            src_ref=stage.at[i, b],
            dst_ref=gat.at[:, columns(c, i)],
            send_sem=out_send.at[i, b],
            recv_sem=out_recv.at[i, c],
            device_id={"ctx": b},
            device_id_type=MESH,
        )

    t_pos = lax.broadcasted_iota(jnp.int32, (rows, rows), 0)
    u_pos = lax.broadcasted_iota(jnp.int32, (rows, rows), 1)
    def add_up():
        for r in range(1, CUBE):
            pltpu.make_async_remote_copy(
                src_ref=decay_in.at[0],
                dst_ref=cums.at[flip(c, r)],
                send_sem=cum_send.at[r],
                recv_sem=cum_recv.at[r],
                device_id={"ctx": flip(c, r)},
                device_id_type=MESH,
            ).wait_recv()

        upto = jnp.where(t_pos <= u_pos, 1.0, 0.0).astype(F32)
        for i in range(per_dev):
            rates = jnp.concatenate(
                [cums[b, pl.ds(head_of(c, i), 1), :] for b in range(CUBE)], axis=0
            )
            sums[i] = jnp.dot(
                rates, upto, preferred_element_type=F32, precision=lax.Precision.HIGHEST
            )

    def decays_of(i, b):
        row = sums[i, pl.ds(b, 1), :]
        col = jnp.sum(jnp.where(t_pos == u_pos, row, 0.0), axis=1, keepdims=True)
        inside = jnp.exp(jnp.where(t_pos >= u_pos, col - row, -jnp.inf))
        return inside, jnp.exp(col), jnp.exp(row[:, rows - 1 :] - col)

    def decays(n, _):
        i, b = n // CUBE, n % CUBE
        inside, opens, closes = decays_of(i, b)
        factors[i, b] = inside
        opening[i, b] = jnp.broadcast_to(opens, (rows, hd))
        closing[i, b] = jnp.broadcast_to(closes, (rows, hd))
        return 0

    def activate(proj):
        qk = jax.nn.silu(proj[:, : 2 * hd]).astype(BF16)
        return jnp.concatenate([qk, proj[:, 2 * hd :].astype(BF16)], axis=1)

    def flipped(r):
        b = c
        bit = 1
        while bit < CUBE:
            b = b + ((r // bit) % 2) * (bit - 2 * bit * ((c // bit) % 2))
            bit *= 2
        return b

    def block_alone(qkv, factor, close):
        q, k, v = qkv[:, :hd], qkv[:, hd : 2 * hd], qkv[:, 2 * hd :]
        scores = lax.dot_general(q, k, (((1,), (1,)), ((), ())), preferred_element_type=F32)
        weights = (scores * factor).astype(BF16)
        inside = jnp.dot(weights, v, preferred_element_type=F32)
        scaled = (k.astype(F32) * close).astype(BF16)
        local = lax.dot_general(scaled, v, (((0,), (0,)), ((), ())), preferred_element_type=F32)
        return inside, local

    def chain(i, b, held, q, inside, local, opens):
        incoming = jnp.dot(q, held.astype(BF16), preferred_element_type=F32) * opens
        total = jnp.exp(sums[i, pl.ds(b, 1), :][:, rows - 1 :])
        state[...] = total * held + local
        stage[i, b] = (inside + incoming).astype(BF16)

    def send(i, b):
        @pl.when(b == c)
        def _():
            gat[:, columns(c, i)] = stage[i, b]

        @pl.when(b != c)
        def _():
            out_copy(i, b).start()

    def near_block(r, _):
        b = flipped(r)
        qkv = activate(jnp.dot(tok[b], w[first], preferred_element_type=F32))
        near_q[b] = qkv[:, :hd]
        near_inside[b], near_local[b] = block_alone(qkv, factors[first, b], closing[first, b])
        return 0

    def piece(b, lo, hi):
        at = pl.ds(lo * step, (hi - lo) * step)
        return jnp.dot(tok[b, :, at], w[far, at, :], preferred_element_type=F32)

    half_way, most = CHUNKS // 2, CHUNKS - CHUNKS // 4

    def grow_first(b, _):
        partial[b] = piece(b, 0, half_way)
        return 0

    def grow_next(b, _):
        partial[b] += piece(b, half_way, most)
        return 0

    def finish(b):
        far_qkv[b % 2] = activate(partial[b] + piece(b, most, CHUNKS))

    def end_plane():
        lax.fori_loop(6, CUBE, near_block, 0)

        state[...] = jnp.zeros_like(state)

        def near_one(b, _):
            given = near_q[b], near_inside[b], near_local[b], opening[first, b]
            chain(first, b, state[...], *given)
            send(first, b)
            return 0

        lax.fori_loop(0, CUBE, near_one, 0)

        end_wait(far, range(half_way))
        lax.fori_loop(0, CUBE, grow_first, 0)
        end_wait(far, range(half_way, most))
        lax.fori_loop(0, CUBE, grow_next, 0)
        end_wait(far, range(most, CHUNKS))

        finish(0)
        state[...] = jnp.zeros_like(state)

        def far_block(b, ahead):
            qkv, held = far_qkv[b % 2], state[...]
            if ahead:
                finish(b + 1)
            inside, local = block_alone(qkv, factors[far, b], closing[far, b])
            chain(far, b, held, qkv[:, :hd], inside, local, opening[far, b])
            send(far, b)

        def far_one(b, _):
            far_block(b, True)
            return 0

        lax.fori_loop(0, CUBE - 1, far_one, 0)
        far_block(CUBE - 1, False)

    def place(t):
        return first + (1 - 2 * first) * (t // CUBE), t % CUBE

    def project(t):
        i, b = place(t)
        return jnp.dot(tok[b], w[i], preferred_element_type=F32)

    def inner_block(t, ahead):
        i, b = place(t)

        @pl.when(b == 0)
        def _():
            state[...] = jnp.zeros_like(state)

        qkv, held = far_qkv[t % 2], state[...]
        proj = project(t + 1) if ahead else None
        factor, opens, closes = decays_of(i, b)
        inside, local = block_alone(qkv, factor, closes)
        chain(i, b, held, qkv[:, :hd], inside, local, opens)
        if ahead:
            far_qkv[(t + 1) % 2] = activate(proj)
        send(i, b)

    def inner_one(t, _):
        inner_block(t, True)
        return 0

    def inner_plane():
        far_qkv[0] = activate(project(0))
        lax.fori_loop(0, per_dev * CUBE - 1, inner_one, 0)
        inner_block(per_dev * CUBE - 1, False)

    inner_pass(first, early)
    tok_wait(2, 0)
    tok_start(2, 0, 4)
    tok_start(2, 0, 1)
    tok_wait(4, 1)
    tok_start(4, 1, 2)
    tok_start(4, 1, 1)
    @pl.when(jnp.logical_not(inner))
    def _():
        add_up()
        lax.fori_loop(0, per_dev * CUBE, decays, 0)

    inner_pass(first, late)
    inner_pass(far, early)
    inner_pass(far, late)
    tok_wait(2, 1)
    tok_start(2, 1, 1)
    tok_wait(4, 0)
    tok_start(4, 0, 1)
    end_wait(first, range(CHUNKS))
    for r in (1, 3, 5):
        for p in (0, 1):
            tok_wait(r, p)
    @pl.when(inner)
    def _():
        add_up()

    @pl.when(jnp.logical_not(inner))
    def _():
        lax.fori_loop(0, 6, near_block, 0)

    tok_wait(6, 0)
    tok_start(6, 0, 1)
    tok_wait(6, 1)
    tok_start(6, 1, 1)
    for p in (0, 1):
        tok_wait(7, p)
    @pl.when(jnp.logical_not(inner))
    def _():
        end_plane()

    @pl.when(inner)
    def _():
        inner_plane()

    for copy in sent:
        copy.wait_send()
    for r in range(1, CUBE):
        cum_copy(r).wait_send()
    for i in range(per_dev):
        for k in range(CHUNKS):

            @pl.when(goes_up(i))
            def _():
                w_copy(i, k, True).wait_send()

            @pl.when(goes_down(i))
            def _():
                w_copy(i, k, False).wait_send()

    for i in range(per_dev):
        for r in range(1, CUBE):
            peer = flip(c, r)
            pltpu.make_async_remote_copy(
                src_ref=stage.at[i, peer],
                dst_ref=gat.at[:, columns(peer, i)],
                send_sem=out_send.at[i, peer],
                recv_sem=out_recv.at[i, peer],
                device_id={"ctx": peer},
                device_id_type=MESH,
            ).wait()

    band = 32

    def norm(n, _):
        at = pl.ds(pl.multiple_of(n * band, band), band)
        x = gat[at, :].astype(F32)
        mean_sq = jnp.sum(x * x, axis=1, keepdims=True) / feats
        out_ref[0, at, :] = (x * lax.rsqrt(mean_sq + 1e-05) * gain_ref[...]).astype(BF16)
        return 0

    lax.fori_loop(0, rows // band, norm, 0)


def head_body(n_ctx, n_fsdp, tokens, qkv_weight, log_decay, norm_gain):
    rows, depth = tokens.shape[1:]
    heads = log_decay.shape[1]
    feats = norm_gain.shape[0]
    hd = feats // heads
    per_dev = heads // n_ctx
    dims = (n_fsdp, heads // n_fsdp, per_dev, hd, feats)
    dma = pltpu.SemaphoreType.DMA
    vmem = pl.BlockSpec(memory_space=pltpu.VMEM)
    hbm = pl.BlockSpec(memory_space=pl.ANY)
    normed = pl.pallas_call(
        functools.partial(head_kernel, dims),
        out_shape=jax.ShapeDtypeStruct((1, rows, feats), BF16),
        in_specs=[hbm, hbm, vmem, vmem],
        out_specs=vmem,
        scratch_shapes=[
            pltpu.VMEM((n_ctx, rows, depth), BF16),
            pltpu.VMEM((per_dev, depth, 3 * hd), BF16),
            pltpu.VMEM((n_ctx, heads, rows), F32),
            pltpu.VMEM((per_dev, n_ctx, rows, hd), BF16),
            pltpu.VMEM((rows, feats), BF16),
            pltpu.VMEM((hd, hd), F32),
            pltpu.VMEM((per_dev, n_ctx, rows), F32),
            pltpu.VMEM((per_dev, n_ctx, rows, rows), F32),
            pltpu.VMEM((per_dev, n_ctx, rows, hd), F32),
            pltpu.VMEM((per_dev, n_ctx, rows, hd), F32),
            pltpu.VMEM((n_ctx, rows, hd), BF16),
            pltpu.VMEM((n_ctx, rows, hd), F32),
            pltpu.VMEM((n_ctx, hd, hd), F32),
            pltpu.VMEM((2, rows, 3 * hd), BF16),
            pltpu.VMEM((n_ctx, rows, 3 * hd), F32),
            dma((4,)),
            dma((CUBE, 2, 3)),
            dma((CUBE, 2)),
            dma((per_dev, CHUNKS)),
            dma((per_dev, CHUNKS)),
            dma((per_dev, CHUNKS)),
            dma((CUBE,)),
            dma((CUBE,)),
            dma((per_dev, n_ctx)),
            dma((per_dev, n_ctx)),
        ],
        compiler_params=pltpu.CompilerParams(
            collective_id=0, has_side_effects=True, vmem_limit_bytes=56 * 1024 * 1024
        ),
        cost_estimate=pl.CostEstimate(
            flops=6 * rows * depth * feats, bytes_accessed=16 * rows * feats, transcendentals=0
        ),
    )(tokens, qkv_weight, log_decay, norm_gain[None])
    return normed


def entering(part, axis, combine, identity):
    place = lax.axis_index(axis)
    gathered = jax.tree.map(lambda a: lax.all_gather(a, axis), part)
    state = jax.tree.map(lambda a, e: jnp.zeros_like(a) + jnp.asarray(e, a.dtype), part, identity)

    def one(turn, state):
        return combine(
            state, jax.tree.map(lambda a: lax.dynamic_index_in_dim(a, turn, 0, False), gathered)
        )

    return lax.fori_loop(0, place, one, state)


def chain_states(decay_total, local):

    def combine(earlier, later):
        return (earlier[0] * later[0], later[0][:, None, None] * earlier[1] + later[1])

    identity_pair = (jnp.ones_like(decay_total), jnp.zeros_like(local))
    return entering((decay_total, local), "ctx", combine, identity_pair)[1]


def segment_memory_matrix(keys, values, cumulative):
    tail = jnp.exp(cumulative[:, -1:] - cumulative)
    weighted_key_vectors = (keys.astype(jnp.float32) * tail.T[:, :, None]).astype(jnp.bfloat16)
    local = jnp.einsum(
        "thd,the->hde", weighted_key_vectors, values, preferred_element_type=jnp.float32
    )
    return (jnp.exp(cumulative[:, -1]), local)


def body(tokens, qkv_weight, log_decay, norm_gain):
    inputs = tokens[0]
    log_rates = log_decay[0]
    head_count = log_rates.shape[0]
    span_len = log_rates.shape[1]
    feat_total = norm_gain.shape[0]
    head_dimension = feat_total // head_count

    def project(piece):
        return jnp.einsum("td,cde->cte", inputs, piece, preferred_element_type=jnp.float32)

    cumulative = jnp.cumsum(log_rates, axis=1)
    paired = project(lax.all_gather(qkv_weight[1:], "fsdp", axis=2, tiled=True))
    keys = jax.nn.silu(paired[0]).astype(jnp.bfloat16).reshape(span_len, head_count, head_dimension)
    values = paired[1].astype(jnp.bfloat16).reshape(span_len, head_count, head_dimension)
    decay_total, local = segment_memory_matrix(keys, values, cumulative)
    carried = chain_states(decay_total, local)
    asked = project(lax.all_gather(qkv_weight[:1], "fsdp", axis=2, tiled=True))
    queries = (
        jax.nn.silu(asked[0]).astype(jnp.bfloat16).reshape(span_len, head_count, head_dimension)
    )
    log_gaps = cumulative[:, :, None] - cumulative[:, None, :]
    causal = jnp.arange(span_len)[:, None] >= jnp.arange(span_len)[None, :]
    factors = jnp.exp(jnp.where(causal[None], log_gaps, -jnp.inf))
    scores = jnp.einsum("thd,shd->hts", queries, keys, preferred_element_type=jnp.float32)
    weights = (scores * factors).astype(jnp.bfloat16)
    inside = jnp.einsum("hts,shd->thd", weights, values, preferred_element_type=jnp.float32)
    reduced_precision_memory = carried.astype(jnp.bfloat16)
    incoming = jnp.einsum(
        "thd,hde->the", queries, reduced_precision_memory, preferred_element_type=jnp.float32
    )
    incoming = incoming * jnp.exp(cumulative).T[:, :, None]
    attention_output = (inside + incoming).reshape(span_len, feat_total)
    mean_sq = jnp.mean(attention_output * attention_output, axis=-1, keepdims=True)
    normed = (attention_output * lax.rsqrt(mean_sq + 1e-05) * norm_gain).astype(jnp.bfloat16)
    return normed[None]


def solution(mesh):
    placed = (P("fsdp", "ctx", None), P(None, None, "fsdp"), P("fsdp", None, "ctx"), P())
    n_ctx, n_fsdp = mesh.shape["ctx"], mesh.shape["fsdp"]

    def run(tokens, qkv_weight, log_decay, norm_gain):
        heads = log_decay.shape[1]
        by_head = n_ctx == CUBE and heads == 2 * n_ctx and n_fsdp % 2 == 0 and heads % n_fsdp == 0
        chosen = functools.partial(head_body, n_ctx, n_fsdp) if by_head else body
        return chosen(tokens, qkv_weight, log_decay, norm_gain)

    return jax.shard_map(
        run, mesh=mesh, in_specs=placed, out_specs=P("fsdp", "ctx", None), check_vma=False
    )
```
